32 devices in a mesh: seq: 8 (over y, x, core), head: 4 (over z).
Axes of the slice: x: 2, y: 2, z: 4, core: 2. Of those that a mesh axis runs over, the one named last changes fastest.
Arguments:
- lin_qkv: bfloat16 [2048, 3, 4096], P('seq', None, 'head'), may hold values from -6 to 6
- resid: bfloat16 [2048, 4096], P('seq', 'head'), may hold values from -6 to 6
- w_out: bfloat16 [4096, 4096], P('head'), may hold values from -0.125 to 0.125
- w_qkv: bfloat16 [4096, 3, 4096], P(None, None, 'head'), may hold values from -2 to 2
Outputs:
- hidden: bfloat16 [2048, 4096], P('seq', 'head')
- attended: bfloat16 [2048, 4096], P('seq', 'head')
The draws below stay inside these ranges and needn't reach their ends.
All inputs are finite; a program needn't handle non-finite values.
Results may differ from the reference program's by a relative error of at most 0.025.
Values may be sent and summed in bfloat16 or wider, within the bound.
No kernel may reach another device: no remote copies, remote signals or barrier semaphores. Data moves between devices by JAX's collectives and lax.ppermute only.
A program may use at most 128 MiB of HBM per device.

```python
import math
import jax
import jax.numpy as jnp
from jax import lax

D = 4096
HEADS = 32
HD = 128
TOK_DEV = 256
TOKENS = 2048
N_SEQ = 8


def draw_w_qkv(key, part):
    limit = 6.0 / math.sqrt(D)
    base = jnp.clip(jax.random.normal(key, (D, 3, HEADS * HD), jnp.float32) / math.sqrt(D), -limit, limit)
    return base.astype(jnp.bfloat16)


def with_spikes(values, stream_key, source, target, blocks, factor):
    def block_of(position):
        return (jnp.arange(values.shape[position]) // (values.shape[position] // blocks)).reshape((-1,) + (1,) * (values.ndim - 1 - position))

    first = jax.random.permutation(stream_key, blocks)[block_of(target)]
    second = (block_of(target) + blocks // 2) % blocks
    return jnp.where((block_of(source) == first) | (block_of(source) == second), factor * values, values)


def steps_of(key, dims, shards, smallest, largest):
    level, own = 1.0, jax.random.fold_in(key, 6)
    for position, blocks in shards:
        draws = jnp.exp(jax.random.uniform(jax.random.fold_in(own, position), (blocks,), jnp.float32, smallest / len(shards), largest / len(shards)))
        level = level * jnp.repeat(draws, dims[position] // blocks).reshape([-1 if axis == position else 1 for axis in range(len(dims))])
    return level


def scatter_about(rng, extent, scale, most, split=(), kind=jnp.bfloat16):
    entries = scale * jax.random.normal(rng, extent, jnp.float32)
    if split:
        entries = entries * steps_of(rng, extent, split, -0.22, 0.18)
    return jnp.clip(entries, -most, most).astype(kind)


def heavy_noise(rng, dims, scale, most, split, heavy, kind=jnp.bfloat16):
    result = scale * jax.random.normal(rng, dims, jnp.float32)
    if split:
        result = result * steps_of(rng, dims, split, -0.22, 0.18)
    return jnp.clip(with_spikes(result, jax.random.fold_in(rng, 3), *heavy), -most, most).astype(kind)


def setup_inputs(seed: int = 0) -> dict:
    splits = jax.random.split(jax.random.key(seed), 5)
    return {
        "lin_qkv": scatter_about(splits[0], (TOKENS, 3, HEADS * HD), 1.0, 6.0, ((0, 8), (2, 4))),
        "resid": scatter_about(splits[1], (TOKENS, D), 1.0, 6.0, ((0, 8), (1, 4))),
        "w_out": heavy_noise(splits[2], (HEADS * HD, D), (HEADS * HD) ** -0.5, 0.125, ((0, 4),), (0, 1, 4, 2.0)),
        "w_qkv": draw_w_qkv(jax.random.fold_in(splits[4], 71), 0),
    }


def rotary(values, positions):
    half = HD // 2
    freq = 500000.0 ** (-(jnp.arange(half, dtype=jnp.float32) * 2.0 / HD))
    angle = positions.astype(jnp.float32)[:, None] * freq[None, :]
    cosine = jnp.cos(angle)[:, None, :]
    sine = jnp.sin(angle)[:, None, :]
    first = values[..., :half]
    second = values[..., half:]
    return jnp.concatenate([first * cosine - second * sine, second * cosine + first * sine], axis=-1)

def reference(lin_qkv, resid, w_out, w_qkv):
    blocks = lin_qkv.reshape(N_SEQ, TOK_DEV, 3, HEADS, HD)

    def kv_state(block):
        keys = block[:, 1].astype(jnp.float32)
        values = block[:, 2].astype(jnp.float32)
        return jnp.einsum('thd,the->hde', keys, values)
    states = lax.map(kv_state, blocks)
    running = jnp.cumsum(states, axis=0)
    prefix = jnp.concatenate([jnp.zeros_like(states[:1]), running[:-1]], axis=0).astype(jnp.bfloat16)
    scale = 1.0 / math.sqrt(HD * TOKENS)
    causal = jnp.tril(jnp.ones((TOK_DEV, TOK_DEV), dtype=bool))

    def lin_block(items):
        block, before = items
        queries = block[:, 0].astype(jnp.float32)
        keys = block[:, 1].astype(jnp.float32)
        values = block[:, 2].astype(jnp.float32)
        scores = jnp.einsum('thd,shd->hts', queries, keys)
        inner = jnp.where(causal[None], scores, 0.0).astype(jnp.bfloat16)
        inner = lax.optimization_barrier(inner).astype(jnp.float32)
        total = jnp.einsum('hts,shd->thd', inner, values) + jnp.einsum('thd,hde->the', queries, before.astype(jnp.float32))
        return (total * scale).astype(jnp.bfloat16)
    lin_out = lax.map(lin_block, (blocks, prefix)).reshape(TOKENS, HEADS * HD)
    mixed_f = resid.astype(jnp.float32) + jnp.dot(lin_out, w_out, preferred_element_type=jnp.float32)
    hidden = mixed_f.astype(jnp.bfloat16)
    meansq = lax.optimization_barrier(jnp.sum(mixed_f * mixed_f, axis=1, keepdims=True)) / D
    normed = (mixed_f * lax.rsqrt(meansq + 1e-05)).astype(jnp.bfloat16)
    proj = jnp.dot(normed, w_qkv.reshape(D, 3 * HEADS * HD), preferred_element_type=jnp.float32)
    proj = proj.reshape(TOKENS, 3, HEADS, HD)
    positions = jnp.arange(TOKENS, dtype=jnp.int32)
    query2 = rotary(proj[:, 0], positions).astype(jnp.bfloat16).reshape(N_SEQ, TOK_DEV, HEADS, HD)
    key2 = rotary(proj[:, 1], positions).astype(jnp.bfloat16).reshape(N_SEQ, TOK_DEV, HEADS, HD)
    value2 = proj[:, 2].astype(jnp.bfloat16).reshape(N_SEQ, TOK_DEV, HEADS, HD)
    key_prev = jnp.concatenate([jnp.zeros_like(key2[:1]), key2[:-1]], axis=0)
    value_prev = jnp.concatenate([jnp.zeros_like(value2[:1]), value2[:-1]], axis=0)
    score_scale = 1.0 / math.sqrt(HD)

    def soft_block(items):
        queries, kprev, vprev, kown, vown, number = items
        keys = jnp.concatenate([kprev, kown], axis=0).astype(jnp.float32)
        values = jnp.concatenate([vprev, vown], axis=0).astype(jnp.float32)
        scores = jnp.einsum('thd,shd->hts', queries.astype(jnp.float32), keys) * score_scale
        allowed = jnp.concatenate([jnp.full((TOK_DEV, TOK_DEV), number > 0), causal], axis=1)
        scores = jnp.where(allowed[None], scores, -1e+30)
        top = lax.optimization_barrier(jnp.max(scores, axis=2, keepdims=True))
        expo = jnp.where(allowed[None], jnp.exp(scores - top), 0.0)
        probs = expo / lax.optimization_barrier(jnp.sum(expo, axis=2, keepdims=True))
        weights = lax.optimization_barrier(probs.astype(jnp.bfloat16)).astype(jnp.float32)
        return jnp.einsum('hts,shd->thd', weights, values).astype(jnp.bfloat16)
    numbers = jnp.arange(N_SEQ, dtype=jnp.int32)
    attended = lax.map(soft_block, (query2, key_prev, value_prev, key2, value2, numbers))
    return (hidden, attended.reshape(TOKENS, HEADS * HD))
```

```python
import functools
import math

import jax
import jax.numpy as jnp
from jax import lax
from jax.experimental import pallas as pl
from jax.experimental.pallas import tpu as pltpu
from jax.sharding import PartitionSpec as P

D = 4096
HD = 128
BF16 = jnp.bfloat16
F32 = jnp.float32
NEG = -1e30

PAIR = [(0, 1), (1, 0), (2, 3), (3, 2)]
CROSS = [(0, 3), (3, 0), (1, 2), (2, 1)]


def shifted(array, axis, by):
    devices = lax.axis_size(axis)
    pairs = [(i, i + by) for i in range(devices) if 0 <= i + by < devices]
    return lax.ppermute(array, axis, pairs)


def swapped(array, axis, bits):
    return lax.ppermute(array, axis, [(i, i ^ bits) for i in range(lax.axis_size(axis))])


def rotary(values, positions):
    half = values.shape[-1] // 2
    freq = 500000.0 ** (-(jnp.arange(half, dtype=jnp.float32) * 2.0 / values.shape[-1]))
    angle = positions.astype(jnp.float32)[:, None] * freq[None, :]
    cosine = jnp.cos(angle)[:, None, :]
    sine = jnp.sin(angle)[:, None, :]
    first = values[..., :half]
    second = values[..., half:]
    return jnp.concatenate(
        [first * cosine - second * sine, second * cosine + first * sine], axis=-1
    )


def general(lin_qkv, resid, w_out, w_qkv):
    tok_rows = lin_qkv.shape[0]
    local_width = lin_qkv.shape[2]
    nheads = local_width // HD
    n_seq = lax.axis_size("seq")
    own_index = lax.axis_index("seq")
    queries = lin_qkv[:, 0].reshape(tok_rows, nheads, HD)
    keys = lin_qkv[:, 1].reshape(tok_rows, nheads, HD)
    values = lin_qkv[:, 2].reshape(tok_rows, nheads, HD)
    own_state = jnp.einsum("thd,the->hde", keys, values, preferred_element_type=jnp.float32)
    piece = lax.all_gather(own_state[None], "seq", axis=0, tiled=True)
    keep = (jnp.arange(piece.shape[0], dtype=jnp.int32) < own_index).astype(jnp.float32)
    before = jnp.sum(piece * keep[:, None, None, None], axis=0)
    before = before.astype(jnp.bfloat16)
    causal = jnp.tril(jnp.ones((tok_rows, tok_rows), dtype=bool))
    scores = jnp.einsum("thd,shd->hts", queries, keys, preferred_element_type=jnp.float32)
    inner = jnp.where(causal[None], scores, 0.0).astype(jnp.bfloat16)
    total = jnp.einsum("hts,shd->thd", inner, values, preferred_element_type=jnp.float32)
    total = total + jnp.einsum("thd,hde->the", queries, before, preferred_element_type=jnp.float32)
    scale = 1.0 / math.sqrt(HD * tok_rows * n_seq)
    lin_out = (total * scale).astype(jnp.bfloat16).reshape(tok_rows, local_width)
    shared = lax.psum_scatter(
        lax.dot_general(
            w_out, lin_out, (((0,), (1,)), ((), ())), preferred_element_type=jnp.float32
        ).astype(jnp.bfloat16),
        "head",
        scatter_dimension=0,
        tiled=True,
    ).astype(jnp.float32)
    mixed_f = resid.astype(jnp.float32) + shared.T
    hidden = mixed_f.astype(jnp.bfloat16)
    flat_w = w_qkv.reshape(w_qkv.shape[0], 3 * local_width)
    squared = lax.psum(jnp.sum(mixed_f * mixed_f, axis=1), "head")
    normed = (mixed_f * lax.rsqrt(squared[:, None] / D + 1e-05)).astype(jnp.bfloat16)
    proj = jnp.dot(
        lax.all_gather(normed, "head", axis=1, tiled=True),
        flat_w,
        preferred_element_type=jnp.float32,
    )
    proj = proj.reshape(tok_rows, 3, nheads, HD)
    positions = own_index * tok_rows + jnp.arange(tok_rows, dtype=jnp.int32)
    query2 = rotary(proj[:, 0], positions).astype(jnp.bfloat16)
    key2 = rotary(proj[:, 1], positions).astype(jnp.bfloat16)
    value2 = proj[:, 2].astype(jnp.bfloat16)
    key_prev, value_prev = shifted((key2, value2), "seq", 1)
    score_scale = 1.0 / math.sqrt(HD)
    all_keys = jnp.concatenate([key_prev, key2], axis=0)
    all_values = jnp.concatenate([value_prev, value2], axis=0)
    logits = (
        jnp.einsum("thd,shd->hts", query2, all_keys, preferred_element_type=jnp.float32)
        * score_scale
    )
    allowed = jnp.concatenate([jnp.full((tok_rows, tok_rows), own_index > 0), causal], axis=1)
    logits = jnp.where(allowed[None], logits, -1e30)
    top = jnp.max(logits, axis=2, keepdims=True)
    expo = jnp.where(allowed[None], jnp.exp(logits - top), 0.0)
    weights = (expo / jnp.sum(expo, axis=2, keepdims=True)).astype(jnp.bfloat16)
    attended = jnp.einsum("hts,shd->thd", weights, all_values, preferred_element_type=jnp.float32)
    return (hidden, attended.astype(jnp.bfloat16).reshape(tok_rows, local_width))


def dot(a, b):
    return jnp.dot(a, b, preferred_element_type=F32)


def dot_nt(a, b):
    return lax.dot_general(a, b, (((1,), (1,)), ((), ())), preferred_element_type=F32)


def dot_tn(a, b):
    return lax.dot_general(a, b, (((0,), (0,)), ((), ())), preferred_element_type=F32)


def head_at(index):
    return pl.ds(pl.multiple_of(index * HD, HD), HD)


def call(body, grid, ins, in_specs, outs, out_specs, scalars=None, scratch=(), vmem=32, flops=0, moved=0):
    return pl.pallas_call(
        body,
        grid_spec=pltpu.PrefetchScalarGridSpec(
            num_scalar_prefetch=1,
            grid=grid,
            in_specs=in_specs,
            out_specs=out_specs,
            scratch_shapes=scratch,
        ),
        out_shape=outs,
        compiler_params=pltpu.CompilerParams(vmem_limit_bytes=vmem * 2**20),
        cost_estimate=pl.CostEstimate(flops=flops, bytes_accessed=moved, transcendentals=0),
    )(scalars, *ins)


def whole(shape):
    return pl.BlockSpec(shape, lambda *_: (0,) * len(shape))


def part(index, rows, width):
    return pl.BlockSpec((None, rows, width), lambda *_: (index, 0, 0))


def state_body(s_ref, k_ref, v_ref, send_ref, keep_ref):
    core = s_ref[0]
    count = send_ref.shape[0]
    for j in range(count):
        for ref, group in ((send_ref, 1 - core), (keep_ref, core)):
            at = head_at(group * count + j)
            ref[j] = dot_tn(k_ref[:, at], v_ref[:, at]).astype(BF16)


def intra_body(s_ref, q_ref, k_ref, v_ref, o_ref):
    rows = q_ref.shape[0]
    ahead = lax.broadcasted_iota(jnp.int32, (rows, rows), 1) > lax.broadcasted_iota(
        jnp.int32, (rows, rows), 0
    )
    for h in range(q_ref.shape[1] // HD):
        at = slice(h * HD, (h + 1) * HD)
        scores = dot_nt(q_ref[:, at], k_ref[:, at])
        inner = jnp.where(ahead, 0.0, scores).astype(BF16)
        o_ref[:, at] = dot(inner, v_ref[:, at])


def send_body(scale, s_ref, q_ref, intra_ref, own_ref, other_ref, w_ref, lin_ref, a_ref, b_ref):
    core = s_ref[0]
    count = own_ref.shape[0]

    @pl.when(pl.program_id(0) == 0)
    def _():
        for j in range(count):
            for ref, group in ((own_ref, core), (other_ref, 1 - core)):
                at = head_at(group * count + j)
                total = intra_ref[:, at] + dot(q_ref[:, at], ref[j])
                lin_ref[:, at] = (total * scale).astype(BF16)

    half = a_ref.shape[0]
    product = dot(lin_ref[...], w_ref[...]).astype(BF16)
    a_ref[...] = product[:half]
    b_ref[...] = product[half:]


def mine_body(per, s_ref, lin_ref, w_ref, r_ref, a_ref, b_ref):
    own = s_ref[4 + pl.program_id(0) // per] == s_ref[1]
    half = a_ref.shape[0]
    product = dot(lin_ref[...], w_ref[...])
    product = product + jnp.where(own, r_ref[...].astype(F32), 0.0)
    product = product.astype(BF16)
    a_ref[...] = product[:half]
    b_ref[...] = product[half:]


def first_body(s_ref, x_ref, w_ref, acc_ref):
    j, k = pl.program_id(0), pl.program_id(1)

    @pl.when(k == 0)
    def _():
        acc_ref[...] = dot(x_ref[...], w_ref[...])

    @pl.when(k > 0)
    def _():
        acc_ref[...] += dot(x_ref[...], w_ref[...])


def second_body(s_ref, x_ref, w_ref, in_ref, t_ref, o_ref, cos_ref, sin_ref, out_ref, acc, inv):
    j, k = pl.program_id(0), pl.program_id(1)

    @pl.when((j == 0) & (k == 0))
    def _():
        t = t_ref[...].astype(F32)
        o = o_ref[...].astype(F32)
        total = jnp.sum(t * t + o * o, axis=1, keepdims=True)
        inv[...] = jnp.broadcast_to(lax.rsqrt(total / D + 1e-05), inv.shape)

    @pl.when(k == 0)
    def _():
        acc[...] = in_ref[...] + dot(x_ref[...], w_ref[...])

    @pl.when(k == pl.num_programs(1) - 1)
    def _():
        cos, sin = cos_ref[...], sin_ref[...]
        for h in range(acc.shape[1] // HD):
            at = slice(h * HD, (h + 1) * HD)
            value = (acc[:, at] + dot(x_ref[...], w_ref[:, at])) * inv[...]
            turned = value * cos + pltpu.roll(value, HD // 2, 1) * sin
            out_ref[:, at] = jnp.where(j == 1, value, turned).astype(BF16)


def attend_body(s_ref, qa_ref, qb_ref, a_ref, b_ref, pa_ref, pb_ref, out_ref):
    has_prev = s_ref[6] > 0
    half = qa_ref.shape[0]
    rows = 2 * half
    row = lax.broadcasted_iota(jnp.int32, (rows, 2 * rows), 0)
    col = lax.broadcasted_iota(jnp.int32, (rows, 2 * rows), 1)
    allowed = ((col < rows) & has_prev) | ((col >= rows) & (col - rows <= row))
    for h in range(qa_ref.shape[1] // HD):
        at = slice(h * HD, (h + 1) * HD)
        queries = jnp.concatenate([qa_ref[:, at], qb_ref[:, at]], axis=0)
        keys = jnp.concatenate([r[0, :, at] for r in (pa_ref, pb_ref, a_ref, b_ref)], axis=0)
        values = jnp.concatenate([r[1, :, at] for r in (pa_ref, pb_ref, a_ref, b_ref)], axis=0)
        logits = dot_nt(queries, keys) * (1.0 / math.sqrt(HD))
        logits = jnp.where(allowed, logits, NEG)
        top = jnp.max(logits, axis=1, keepdims=True)
        expo = jnp.where(allowed, jnp.exp(logits - top), 0.0)
        weights = (expo / jnp.sum(expo, axis=1, keepdims=True)).astype(BF16)
        out_ref[:, at] = dot(weights, values).astype(BF16)


def tuned(lin_qkv, resid, w_out, w_qkv):
    rows, _, width = lin_qkv.shape
    nheads = width // HD
    half = rows // 2
    group = nheads // 2
    full = w_out.shape[1]
    seq = lax.axis_index("seq").astype(jnp.int32)
    z = lax.axis_index("head").astype(jnp.int32)
    core = seq % 2
    edge = (z == 0) | (z == 3)
    order = jnp.where(edge, jnp.array([1, 2, 0, 3], jnp.int32), jnp.array([0, 3, 1, 2], jnp.int32))
    scalars = jnp.concatenate([jnp.stack([core, z]), order, jnp.stack([seq, z // 2])])

    qkv = jnp.transpose(lin_qkv, (1, 0, 2))
    wqkv = jnp.transpose(w_qkv, (1, 0, 2))
    heads = lambda n: jax.ShapeDtypeStruct((n, HD, HD), BF16)
    q_spec, k_spec, v_spec = (part(i, rows, width) for i in range(3))

    with jax.named_scope("state"):
        send, keep = call(
            state_body, (1,), (qkv, qkv), [k_spec, v_spec],
            (heads(group), heads(group)), (whole((group, HD, HD)),) * 2,
            scalars, flops=2 * rows * width * HD, moved=4 * rows * width,
        )
        other = swapped(send, "seq", 1)
        chip_total = (keep.astype(F32) + other.astype(F32)).astype(BF16)
        by_x = swapped(chip_total, "seq", 2)
        by_y = swapped(chip_total, "seq", 4)
        by_xy = swapped(chip_total, "seq", 6)
    with jax.named_scope("intra"):
        intra = call(
            intra_body, (1,), (qkv, qkv, qkv), [q_spec, k_spec, v_spec],
            jax.ShapeDtypeStruct((rows, width), F32), whole((rows, width)),
            scalars, flops=4 * rows * rows * width, moved=10 * rows * width,
        )
    with jax.named_scope("prefix"):
        x_bit = ((seq // 2) % 2).astype(F32)
        y_bit = (seq // 4).astype(F32)
        chips = (
            by_x.astype(F32) * x_bit + by_y.astype(F32) * y_bit + by_xy.astype(F32) * y_bit
        )
        low = chips.astype(BF16)
        first_core = jnp.where(core == 0, keep, other)
        high = (chips + first_core.astype(F32)).astype(BF16)
        own_prefix = jnp.where(core == 0, low, high)
        other_prefix = swapped(jnp.where(core == 0, high, low), "seq", 1)

    scale = 1.0 / math.sqrt(HD * rows * lax.axis_size("seq"))
    block = width // 2
    per = width // block
    w_at = lambda base: pl.BlockSpec(
        (width, block), lambda i, s: (0, s[base + i // per] * per + i % per)
    )
    half_out = pl.BlockSpec((half, block), lambda i, s: (0, i))
    halves = jax.ShapeDtypeStruct((half, full // 2), BF16)
    with jax.named_scope("partials"):
        lin_out, send_a, send_b = call(
            functools.partial(send_body, scale), (2 * per,),
            (qkv, intra, own_prefix, other_prefix, w_out),
            [q_spec, whole((rows, width)), whole((group, HD, HD)), whole((group, HD, HD)), w_at(2)],
            (jax.ShapeDtypeStruct((rows, width), BF16), halves, halves),
            (whole((rows, width)), half_out, half_out),
            scalars, flops=rows * width * full, moved=width * full,
        )
        got_a = lax.ppermute(send_a, "head", PAIR)
        mine_a, mine_b = call(
            functools.partial(mine_body, per), (2 * per,), (lin_out, w_out, resid),
            [whole((rows, width)), w_at(4), pl.BlockSpec((rows, block), lambda i, s: (0, i % per))],
            (halves, halves), (half_out, half_out),
            scalars, flops=rows * width * full, moved=width * full,
        )

    positions = seq * rows + jnp.arange(rows, dtype=jnp.int32)
    freq = 500000.0 ** (-(jnp.arange(HD // 2, dtype=F32) * 2.0 / HD))
    angle = positions.astype(F32)[:, None] * freq[None, :]
    cosine, sine = jnp.cos(angle), jnp.sin(angle)
    cos2 = jnp.concatenate([cosine, cosine], axis=1)
    sin2 = jnp.concatenate([-sine, sine], axis=1)

    def w_rows(base):
        return pl.BlockSpec(
            (None, width, width), lambda j, k, s: ((j + 1) % 3, s[base + k], 0)
        )

    x_spec = pl.BlockSpec((half, width), lambda j, k, s: (0, k))
    acc_spec = pl.BlockSpec((None, half, width), lambda j, k, s: (j, 0, 0))

    def own_part(total):
        return call(
            first_body, (3, 2), (total, wqkv), [x_spec, w_rows(4)],
            jax.ShapeDtypeStruct((3, half, width), F32), acc_spec,
            scalars, flops=half * full * 3 * width, moved=3 * width * full,
        )

    def rest(total, got, acc, index):
        turn = pl.BlockSpec((half, HD), lambda *_: (index, 0))
        return call(
            second_body, (3, 2), (got, wqkv, acc, total, got, cos2, sin2),
            [x_spec, w_rows(2), acc_spec, whole((half, full // 2)), whole((half, full // 2)), turn, turn],
            jax.ShapeDtypeStruct((3, half, width), BF16), acc_spec,
            scalars, scratch=(pltpu.VMEM((half, width), F32), pltpu.VMEM((half, HD), F32)),
            flops=half * full * 3 * width, moved=3 * width * full,
        )

    def add(a, b):
        return (a.astype(F32) + b.astype(F32)).astype(BF16)

    with jax.named_scope("mix"):
        send_b, got_a = lax.optimization_barrier((send_b, got_a))
        got_b = lax.ppermute(send_b, "head", PAIR)
        sum_a = add(mine_a, got_a)
        far_a = lax.ppermute(sum_a, "head", CROSS)
        sum_b = add(mine_b, got_b)
        far_b = lax.ppermute(sum_b, "head", CROSS)
        total_a = add(sum_a, far_a)
        rest_a = lax.ppermute(total_a, "head", PAIR)
        total_b = add(sum_b, far_b)
        rest_b = lax.ppermute(total_b, "head", PAIR)
    with jax.named_scope("project_a"):
        kvq_a = rest(total_a, rest_a, own_part(total_a), 0)
        prev_a = shifted(kvq_a[:2], "seq", 1)
    with jax.named_scope("project_b"):
        kvq_b = rest(total_b, rest_b, own_part(total_b), 1)
        prev_b = shifted(kvq_b[:2], "seq", 1)
    hidden = jnp.concatenate([total_a, total_b], axis=0)
    hidden = jnp.where(z < 2, hidden[:, :width], hidden[:, width:])
    with jax.named_scope("attend"):
        kv = whole((2, half, width))
        q2 = part(2, half, width)
        attended = call(
            attend_body, (1,), (kvq_a, kvq_b, kvq_a, kvq_b, prev_a, prev_b),
            [q2, q2, kv, kv, kv, kv],
            jax.ShapeDtypeStruct((rows, width), BF16), whole((rows, width)),
            scalars, flops=8 * rows * rows * width, moved=12 * rows * width,
        )
    return hidden, attended


def solution(mesh):
    line = mesh.shape["seq"] == 8 and mesh.shape["head"] == 4
    return jax.shard_map(
        tuned if line else general,
        mesh=mesh,
        in_specs=(P("seq", None, "head"), P("seq", "head"), P("head", None), P(None, None, "head")),
        out_specs=(P("seq", "head"), P("seq", "head")),
        check_vma=False,
    )
```

```python
import functools
import math

import jax
import jax.numpy as jnp
from jax import lax
from jax.experimental import pallas as pl
from jax.experimental.pallas import tpu as pltpu
from jax.sharding import PartitionSpec as P

D = 4096
HD = 128
BF16 = jnp.bfloat16
F32 = jnp.float32
NEG = -1e30

PAIR = [(0, 1), (1, 0), (2, 3), (3, 2)]
CROSS = [(0, 3), (3, 0), (1, 2), (2, 1)]


def shifted(array, axis, by):
    devices = lax.axis_size(axis)
    pairs = [(i, i + by) for i in range(devices) if 0 <= i + by < devices]
    return lax.ppermute(array, axis, pairs)


def swapped(array, axis, bits):
    return lax.ppermute(array, axis, [(i, i ^ bits) for i in range(lax.axis_size(axis))])


def rotary(values, positions):
    half = values.shape[-1] // 2
    freq = 500000.0 ** (-(jnp.arange(half, dtype=jnp.float32) * 2.0 / values.shape[-1]))
    angle = positions.astype(jnp.float32)[:, None] * freq[None, :]
    cosine = jnp.cos(angle)[:, None, :]
    sine = jnp.sin(angle)[:, None, :]
    first = values[..., :half]
    second = values[..., half:]
    return jnp.concatenate(
        [first * cosine - second * sine, second * cosine + first * sine], axis=-1
    )


def general(lin_qkv, resid, w_out, w_qkv):
    tok_rows = lin_qkv.shape[0]
    local_width = lin_qkv.shape[2]
    nheads = local_width // HD
    n_seq = lax.axis_size("seq")
    own_index = lax.axis_index("seq")
    queries = lin_qkv[:, 0].reshape(tok_rows, nheads, HD)
    keys = lin_qkv[:, 1].reshape(tok_rows, nheads, HD)
    values = lin_qkv[:, 2].reshape(tok_rows, nheads, HD)
    own_state = jnp.einsum("thd,the->hde", keys, values, preferred_element_type=jnp.float32)
    piece = lax.all_gather(own_state[None], "seq", axis=0, tiled=True)
    keep = (jnp.arange(piece.shape[0], dtype=jnp.int32) < own_index).astype(jnp.float32)
    before = jnp.sum(piece * keep[:, None, None, None], axis=0)
    before = before.astype(jnp.bfloat16)
    causal = jnp.tril(jnp.ones((tok_rows, tok_rows), dtype=bool))
    scores = jnp.einsum("thd,shd->hts", queries, keys, preferred_element_type=jnp.float32)
    inner = jnp.where(causal[None], scores, 0.0).astype(jnp.bfloat16)
    total = jnp.einsum("hts,shd->thd", inner, values, preferred_element_type=jnp.float32)
    total = total + jnp.einsum("thd,hde->the", queries, before, preferred_element_type=jnp.float32)
    scale = 1.0 / math.sqrt(HD * tok_rows * n_seq)
    lin_out = (total * scale).astype(jnp.bfloat16).reshape(tok_rows, local_width)
    shared = lax.psum_scatter(
        lax.dot_general(
            w_out, lin_out, (((0,), (1,)), ((), ())), preferred_element_type=jnp.float32
        ).astype(jnp.bfloat16),
        "head",
        scatter_dimension=0,
        tiled=True,
    ).astype(jnp.float32)
    mixed_f = resid.astype(jnp.float32) + shared.T
    hidden = mixed_f.astype(jnp.bfloat16)
    flat_w = w_qkv.reshape(w_qkv.shape[0], 3 * local_width)
    squared = lax.psum(jnp.sum(mixed_f * mixed_f, axis=1), "head")
    normed = (mixed_f * lax.rsqrt(squared[:, None] / D + 1e-05)).astype(jnp.bfloat16)
    proj = jnp.dot(
        lax.all_gather(normed, "head", axis=1, tiled=True),
        flat_w,
        preferred_element_type=jnp.float32,
    )
    proj = proj.reshape(tok_rows, 3, nheads, HD)
    positions = own_index * tok_rows + jnp.arange(tok_rows, dtype=jnp.int32)
    query2 = rotary(proj[:, 0], positions).astype(jnp.bfloat16)
    key2 = rotary(proj[:, 1], positions).astype(jnp.bfloat16)
    value2 = proj[:, 2].astype(jnp.bfloat16)
    key_prev, value_prev = shifted((key2, value2), "seq", 1)
    score_scale = 1.0 / math.sqrt(HD)
    all_keys = jnp.concatenate([key_prev, key2], axis=0)
    all_values = jnp.concatenate([value_prev, value2], axis=0)
    logits = (
        jnp.einsum("thd,shd->hts", query2, all_keys, preferred_element_type=jnp.float32)
        * score_scale
    )
    allowed = jnp.concatenate([jnp.full((tok_rows, tok_rows), own_index > 0), causal], axis=1)
    logits = jnp.where(allowed[None], logits, -1e30)
    top = jnp.max(logits, axis=2, keepdims=True)
    expo = jnp.where(allowed[None], jnp.exp(logits - top), 0.0)
    weights = (expo / jnp.sum(expo, axis=2, keepdims=True)).astype(jnp.bfloat16)
    attended = jnp.einsum("hts,shd->thd", weights, all_values, preferred_element_type=jnp.float32)
    return (hidden, attended.astype(jnp.bfloat16).reshape(tok_rows, local_width))


def dot(a, b):
    return jnp.dot(a, b, preferred_element_type=F32)


def dot_nt(a, b):
    return lax.dot_general(a, b, (((1,), (1,)), ((), ())), preferred_element_type=F32)


def dot_tn(a, b):
    return lax.dot_general(a, b, (((0,), (0,)), ((), ())), preferred_element_type=F32)


def at(start, size):
    return pl.ds(pl.multiple_of(start, size), size)


ON_CHIP = pl.BlockSpec(memory_space=pltpu.VMEM)
IN_HBM = pl.BlockSpec(memory_space=pltpu.HBM)
ANYWHERE = pl.BlockSpec(memory_space=pl.ANY)


def call(body, ins, outs, in_specs=None, scratch=(), vmem=20, flops=0, moved=0):
    return pl.pallas_call(
        body,
        in_specs=in_specs or [ON_CHIP] * len(ins),
        out_specs=jax.tree.map(lambda _: ON_CHIP, outs),
        out_shape=outs,
        scratch_shapes=scratch,
        compiler_params=pltpu.CompilerParams(vmem_limit_bytes=vmem * 2**20),
        cost_estimate=pl.CostEstimate(flops=flops, bytes_accessed=moved, transcendentals=0),
    )(*ins)


def load_body(source, after, target, sems):
    copies = []
    for i in range(sems.shape[0]):
        copy = pltpu.make_async_copy(source.at[i], target.at[i], sems.at[i])
        copy.start()
        copies.append(copy)
    for copy in copies:
        copy.wait()


def loaded(array, after):
    return call(
        load_body, (array, after), pltpu.VMEM(array.shape, array.dtype),
        [IN_HBM, ANYWHERE], (pltpu.SemaphoreType.DMA((array.shape[0],)),), vmem=4, moved=2 * array.size,
    )


def state_body(qkv_ref, send_ref, keep_ref, k_ref, v_ref, sems):
    core = lax.axis_index("seq") % 2
    count = send_ref.shape[0]
    wide = k_ref.shape[2]
    copies = []
    for slot in range(2):
        group = core if slot else 1 - core
        pair = []
        for plane, ref in ((1, k_ref), (2, v_ref)):
            copy = pltpu.make_async_copy(
                qkv_ref.at[plane, :, at(group * wide, wide)], ref.at[slot], sems.at[slot, plane - 1]
            )
            copy.start()
            pair.append(copy)
        copies.append(pair)
    for slot, out in ((0, send_ref), (1, keep_ref)):
        for copy in copies[slot]:
            copy.wait()
        for j in range(count):
            head = slice(j * HD, (j + 1) * HD)
            out[j] = dot_tn(k_ref[slot, :, head], v_ref[slot, :, head]).astype(BF16)


def intra_body(qkv_ref, o_ref, q_ref):
    rows = qkv_ref.shape[1]
    ahead = lax.broadcasted_iota(jnp.int32, (rows, rows), 1) > lax.broadcasted_iota(
        jnp.int32, (rows, rows), 0
    )
    q_ref[...] = qkv_ref[0]
    for h in range(qkv_ref.shape[2] // HD):
        head = slice(h * HD, (h + 1) * HD)
        scores = dot_nt(qkv_ref[0, :, head], qkv_ref[1, :, head])
        inner = jnp.where(ahead, 0.0, scores).astype(BF16)
        o_ref[:, head] = dot(inner, qkv_ref[2, :, head])


def quarters():
    z = lax.axis_index("head")
    edge = (z == 0) | (z == 3)
    outer, inner = (0, 3), (1, 2)
    mine = [jnp.where(edge, a, b) for a, b in zip(outer, inner)]
    other = [jnp.where(edge, b, a) for a, b in zip(outer, inner)]
    return z, mine, other


def send_body(scale, q_ref, intra_ref, own_ref, other_ref, w_ref, lin_ref, a_ref, b_ref):
    core = lax.axis_index("seq") % 2
    count = own_ref.shape[0]
    for ref, group in ((own_ref, core), (other_ref, 1 - core)):
        for j in range(count):
            head = at((group * count + j) * HD, HD)
            total = intra_ref[:, head] + dot(q_ref[:, head], ref[j])
            lin_ref[:, head] = (total * scale).astype(BF16)
    _, _, other = quarters()
    half, width = a_ref.shape[0], a_ref.shape[1] // 2
    block = width // 2
    for p in range(2):
        for n in range(2):
            product = dot(lin_ref[...], w_ref[:, at(other[p] * width + n * block, block)]).astype(BF16)
            to = slice(p * width + n * block, p * width + (n + 1) * block)
            a_ref[:, to] = product[:half]
            b_ref[:, to] = product[half:]


def mine_body(lin_ref, w_ref, r_ref, a_ref, b_ref):
    z, mine, _ = quarters()
    half, width = a_ref.shape[0], a_ref.shape[1] // 2
    block = width // 2
    for p in range(2):
        for n in range(2):
            product = dot(lin_ref[...], w_ref[:, at(mine[p] * width + n * block, block)])
            own = r_ref[:, n * block : (n + 1) * block].astype(F32)
            product = (product + jnp.where(mine[p] == z, own, 0.0)).astype(BF16)
            to = slice(p * width + n * block, p * width + (n + 1) * block)
            a_ref[:, to] = product[:half]
            b_ref[:, to] = product[half:]


def two_quarters(x_ref, w_ref, plane, which, to):
    width = x_ref.shape[1] // 2
    low = dot(x_ref[:, :width], w_ref[plane, at(which[0] * width, width), to])
    return low + dot(x_ref[:, width:], w_ref[plane, at(which[1] * width, width), to])


def first_body(block, x_ref, w_ref, acc_ref):
    _, mine, _ = quarters()
    for plane in range(3):
        for n in range(acc_ref.shape[2] // block):
            to = slice(n * block, (n + 1) * block)
            acc_ref[plane, :, to] = two_quarters(x_ref, w_ref, plane, mine, to)


def first_hidden_body(block, x_ref, w_ref, a_ref, acc_ref, hidden_ref):
    half, width = a_ref.shape[0], a_ref.shape[1] // 2
    own = at((lax.axis_index("head") // 2) * width, width)
    hidden_ref[:half] = a_ref[:, own]
    hidden_ref[half:] = x_ref[:, own]
    first_body(block, x_ref, w_ref, acc_ref)


def finish(block, plane, x_ref, w_ref, acc_ref, inv, cos, sin, out_ref):
    _, _, other = quarters()
    for n in range(acc_ref.shape[2] // block):
        to = slice(n * block, (n + 1) * block)
        total = (acc_ref[plane, :, to] + two_quarters(x_ref, w_ref, plane, other, to)) * inv
        if plane == 2:
            out_ref[:, to] = total.astype(BF16)
            continue
        for h in range(block // HD):
            value = total[:, h * HD : (h + 1) * HD]
            turned = value * cos + pltpu.roll(value, HD // 2, 1) * sin
            out_ref[:, n * block + h * HD : n * block + (h + 1) * HD] = turned.astype(BF16)


def kv_body(block, t_ref, x_ref, w_ref, acc_ref, cos_ref, sin_ref, kv_ref, inv_ref):
    t = t_ref[...].astype(F32)
    x = x_ref[...].astype(F32)
    total = jnp.sum(t * t + x * x, axis=1, keepdims=True)
    inv = lax.rsqrt(total / D + 1e-05)
    inv_ref[...] = jnp.broadcast_to(inv, inv_ref.shape)
    for plane in (1, 2):
        finish(block, plane, x_ref, w_ref, acc_ref, inv, cos_ref[...], sin_ref[...], kv_ref.at[plane - 1])


def q_body(block, x_ref, w_ref, acc_ref, inv_ref, cos_ref, sin_ref, q_ref):
    inv = inv_ref[:, :1]
    finish(block, 0, x_ref, w_ref, acc_ref, inv, cos_ref[...], sin_ref[...], q_ref)


SCORE = 1.0 / math.sqrt(HD)


def early_body(qa_ref, qb_ref, a_ref, b_ref, pa_ref, acc_ref, top_ref, sum_ref):
    has_prev = lax.axis_index("seq") > 0
    half = qa_ref.shape[0]
    shape = (2 * half, 3 * half)
    row = lax.broadcasted_iota(jnp.int32, shape, 0)
    col = lax.broadcasted_iota(jnp.int32, shape, 1)
    allowed = ((col < half) & has_prev) | ((col >= half) & (col - half <= row))
    for h in range(qa_ref.shape[1] // HD):
        head = slice(h * HD, (h + 1) * HD)
        queries = jnp.concatenate([qa_ref[:, head], qb_ref[:, head]], axis=0)
        keys = jnp.concatenate([r[0, :, head] for r in (pa_ref, a_ref, b_ref)], axis=0)
        values = jnp.concatenate([r[1, :, head] for r in (pa_ref, a_ref, b_ref)], axis=0)
        logits = jnp.where(allowed, dot_nt(queries, keys) * SCORE, NEG)
        top = jnp.max(logits, axis=1, keepdims=True)
        expo = jnp.where(allowed, jnp.exp(logits - top), 0.0)
        top_ref[h] = top
        sum_ref[h] = jnp.sum(expo, axis=1, keepdims=True)
        acc_ref[:, head] = dot(expo.astype(BF16), values)


def late_body(qa_ref, qb_ref, pb_ref, acc_ref, top_ref, sum_ref, out_ref):
    has_prev = lax.axis_index("seq") > 0
    for h in range(qa_ref.shape[1] // HD):
        head = slice(h * HD, (h + 1) * HD)
        queries = jnp.concatenate([qa_ref[:, head], qb_ref[:, head]], axis=0)
        logits = jnp.where(has_prev, dot_nt(queries, pb_ref[0, :, head]) * SCORE, NEG)
        before = top_ref[h]
        top = jnp.maximum(before, jnp.max(logits, axis=1, keepdims=True))
        expo = jnp.where(has_prev, jnp.exp(logits - top), 0.0)
        fade = jnp.exp(before - top)
        total = sum_ref[h] * fade + jnp.sum(expo, axis=1, keepdims=True)
        acc = acc_ref[:, head] * fade + dot(expo.astype(BF16), pb_ref[1, :, head])
        out_ref[:, head] = (acc / total).astype(BF16)


def tuned(lin_qkv, resid, w_out, w_qkv):
    rows, _, width = lin_qkv.shape
    nheads = width // HD
    half = rows // 2
    group = nheads // 2
    full = w_out.shape[1]
    block = width // 2
    seq = lax.axis_index("seq")
    core = seq % 2
    shape = jax.ShapeDtypeStruct

    qkv = jnp.transpose(lin_qkv, (1, 0, 2))
    wqkv = jnp.transpose(w_qkv, (1, 0, 2))

    with jax.named_scope("state"):
        states = shape((group, HD, HD), BF16)
        send, keep = call(
            state_body, (qkv,), (states, states), [IN_HBM],
            (
                pltpu.VMEM((2, rows, width // 2), BF16),
                pltpu.VMEM((2, rows, width // 2), BF16),
                pltpu.SemaphoreType.DMA((2, 2)),
            ),
            flops=2 * rows * width * HD, moved=4 * rows * width,
        )
        other = swapped(send, "seq", 1)
        chip_total = (keep.astype(F32) + other.astype(F32)).astype(BF16)
        by_x = swapped(chip_total, "seq", 2)
        by_y = swapped(chip_total, "seq", 4)
        by_xy = swapped(chip_total, "seq", 6)
    with jax.named_scope("intra"):
        intra, q = call(
            intra_body, (qkv,), (shape((rows, width), F32), shape((rows, width), BF16)),
            flops=4 * rows * rows * width, moved=10 * rows * width,
        )
    with jax.named_scope("load_w_out"):
        w_out_here = loaded(w_out.reshape(4, width // 4, full), chip_total).reshape(width, full)
    with jax.named_scope("prefix"):
        x_bit = ((seq // 2) % 2).astype(F32)
        y_bit = (seq // 4).astype(F32)
        chips = (
            by_x.astype(F32) * x_bit + by_y.astype(F32) * y_bit + by_xy.astype(F32) * y_bit
        )
        low = chips.astype(BF16)
        first_core = jnp.where(core == 0, keep, other)
        high = (chips + first_core.astype(F32)).astype(BF16)
        own_prefix = jnp.where(core == 0, low, high)
        other_prefix = swapped(jnp.where(core == 0, high, low), "seq", 1)

    scale = 1.0 / math.sqrt(HD * rows * lax.axis_size("seq"))
    halves = shape((half, full // 2), BF16)
    with jax.named_scope("partials"):
        lin_out, send_a, send_b = call(
            functools.partial(send_body, scale), (q, intra, own_prefix, other_prefix, w_out_here),
            (shape((rows, width), BF16), halves, halves), flops=rows * width * full, moved=width * full,
        )
        got_a = lax.ppermute(send_a, "head", PAIR)
        mine_a, mine_b = call(
            mine_body, (lin_out, w_out_here, resid), (halves, halves),
            flops=rows * width * full, moved=width * full,
        )
    with jax.named_scope("load_w_qkv"):
        w_here = loaded(wqkv.reshape(3, 4, width, width).reshape(12, width, width), mine_a)
        w_here = w_here.reshape(3, full, width)

    positions = seq * rows + jnp.arange(rows, dtype=jnp.int32)
    freq = 500000.0 ** (-(jnp.arange(HD // 2, dtype=F32) * 2.0 / HD))
    angle = positions.astype(F32)[:, None] * freq[None, :]
    cosine, sine = jnp.cos(angle), jnp.sin(angle)
    cos2 = jnp.concatenate([cosine, cosine], axis=1)
    sin2 = jnp.concatenate([-sine, sine], axis=1)

    accs = shape((3, half, width), F32)
    cost = dict(flops=half * full * 3 * width, moved=3 * width * full)

    def add(a, b):
        return (a.astype(F32) + b.astype(F32)).astype(BF16)

    def project(total, got, acc, index):
        turn = (cos2[index * half : (index + 1) * half], sin2[index * half : (index + 1) * half])
        kv, inv = call(
            functools.partial(kv_body, block), (total, got, w_here, acc, *turn),
            (shape((2, half, width), BF16), shape((half, HD), F32)), **cost,
        )
        before = shifted(kv, "seq", 1)
        query = call(
            functools.partial(q_body, block), (got, w_here, acc, inv, *turn), shape((half, width), BF16), **cost,
        )
        return kv, before, query

    with jax.named_scope("mix"):
        send_b, got_a = lax.optimization_barrier((send_b, got_a))
        got_b = lax.ppermute(send_b, "head", PAIR)
        sum_a = add(mine_a, got_a)
        far_a = lax.ppermute(sum_a, "head", CROSS)
        sum_b = add(mine_b, got_b)
        sum_b, far_a = lax.optimization_barrier((sum_b, far_a))
        far_b = lax.ppermute(sum_b, "head", CROSS)
        total_a = add(sum_a, far_a)
        rest_a = lax.ppermute(total_a, "head", PAIR)
        total_b = add(sum_b, far_b)
        rest_b = lax.ppermute(total_b, "head", PAIR)
    with jax.named_scope("project_a"):
        acc_a = call(functools.partial(first_body, block), (total_a, w_here), accs, **cost)
        kv_a, prev_a, query_a = project(total_a, rest_a, acc_a, 0)
    with jax.named_scope("project_b"):
        acc_b, hidden = call(
            functools.partial(first_hidden_body, block), (total_b, w_here, total_a),
            (accs, shape((rows, width), BF16)), **cost,
        )
        kv_b, prev_b, query_b = project(total_b, rest_b, acc_b, 1)
    with jax.named_scope("attend"):
        stat = shape((nheads, rows, 1), F32)
        acc, top, total = call(
            early_body, (query_a, query_b, kv_a, kv_b, prev_a), (shape((rows, width), F32), stat, stat),
            flops=6 * rows * rows * width, moved=12 * rows * width,
        )
        attended = call(
            late_body, (query_a, query_b, prev_b, acc, top, total), shape((rows, width), BF16),
            flops=2 * rows * rows * width, moved=12 * rows * width,
        )
    return hidden, attended


def solution(mesh):
    line = mesh.shape["seq"] == 8 and mesh.shape["head"] == 4
    return jax.shard_map(
        tuned if line else general,
        mesh=mesh,
        in_specs=(P("seq", None, "head"), P("seq", "head"), P("head", None), P(None, None, "head")),
        out_specs=(P("seq", "head"), P("seq", "head")),
        check_vma=False,
    )
```

```python
import functools
import math

import jax
import jax.numpy as jnp
from jax import lax
from jax.experimental import pallas as pl
from jax.experimental.pallas import tpu as pltpu
from jax.sharding import PartitionSpec as P

D = 4096
HD = 128
BF16 = jnp.bfloat16
F32 = jnp.float32
NEG = -1e30

PAIR = [(0, 1), (1, 0), (2, 3), (3, 2)]
CROSS = [(0, 3), (3, 0), (1, 2), (2, 1)]


def shifted(array, axis, by):
    devices = lax.axis_size(axis)
    pairs = [(i, i + by) for i in range(devices) if 0 <= i + by < devices]
    return lax.ppermute(array, axis, pairs)


def swapped(array, axis, bits):
    return lax.ppermute(array, axis, [(i, i ^ bits) for i in range(lax.axis_size(axis))])


def rotary(values, positions):
    half = values.shape[-1] // 2
    freq = 500000.0 ** (-(jnp.arange(half, dtype=jnp.float32) * 2.0 / values.shape[-1]))
    angle = positions.astype(jnp.float32)[:, None] * freq[None, :]
    cosine = jnp.cos(angle)[:, None, :]
    sine = jnp.sin(angle)[:, None, :]
    first = values[..., :half]
    second = values[..., half:]
    return jnp.concatenate(
        [first * cosine - second * sine, second * cosine + first * sine], axis=-1
    )


def general(lin_qkv, resid, w_out, w_qkv):
    tok_rows = lin_qkv.shape[0]
    local_width = lin_qkv.shape[2]
    nheads = local_width // HD
    n_seq = lax.axis_size("seq")
    own_index = lax.axis_index("seq")
    queries = lin_qkv[:, 0].reshape(tok_rows, nheads, HD)
    keys = lin_qkv[:, 1].reshape(tok_rows, nheads, HD)
    values = lin_qkv[:, 2].reshape(tok_rows, nheads, HD)
    own_state = jnp.einsum("thd,the->hde", keys, values, preferred_element_type=jnp.float32)
    piece = lax.all_gather(own_state[None], "seq", axis=0, tiled=True)
    keep = (jnp.arange(piece.shape[0], dtype=jnp.int32) < own_index).astype(jnp.float32)
    before = jnp.sum(piece * keep[:, None, None, None], axis=0)
    before = before.astype(jnp.bfloat16)
    causal = jnp.tril(jnp.ones((tok_rows, tok_rows), dtype=bool))
    scores = jnp.einsum("thd,shd->hts", queries, keys, preferred_element_type=jnp.float32)
    inner = jnp.where(causal[None], scores, 0.0).astype(jnp.bfloat16)
    total = jnp.einsum("hts,shd->thd", inner, values, preferred_element_type=jnp.float32)
    total = total + jnp.einsum("thd,hde->the", queries, before, preferred_element_type=jnp.float32)
    scale = 1.0 / math.sqrt(HD * tok_rows * n_seq)
    lin_out = (total * scale).astype(jnp.bfloat16).reshape(tok_rows, local_width)
    shared = lax.psum_scatter(
        lax.dot_general(
            w_out, lin_out, (((0,), (1,)), ((), ())), preferred_element_type=jnp.float32
        ).astype(jnp.bfloat16),
        "head",
        scatter_dimension=0,
        tiled=True,
    ).astype(jnp.float32)
    mixed_f = resid.astype(jnp.float32) + shared.T
    hidden = mixed_f.astype(jnp.bfloat16)
    flat_w = w_qkv.reshape(w_qkv.shape[0], 3 * local_width)
    squared = lax.psum(jnp.sum(mixed_f * mixed_f, axis=1), "head")
    normed = (mixed_f * lax.rsqrt(squared[:, None] / D + 1e-05)).astype(jnp.bfloat16)
    proj = jnp.dot(
        lax.all_gather(normed, "head", axis=1, tiled=True),
        flat_w,
        preferred_element_type=jnp.float32,
    )
    proj = proj.reshape(tok_rows, 3, nheads, HD)
    positions = own_index * tok_rows + jnp.arange(tok_rows, dtype=jnp.int32)
    query2 = rotary(proj[:, 0], positions).astype(jnp.bfloat16)
    key2 = rotary(proj[:, 1], positions).astype(jnp.bfloat16)
    value2 = proj[:, 2].astype(jnp.bfloat16)
    key_prev, value_prev = shifted((key2, value2), "seq", 1)
    score_scale = 1.0 / math.sqrt(HD)
    all_keys = jnp.concatenate([key_prev, key2], axis=0)
    all_values = jnp.concatenate([value_prev, value2], axis=0)
    logits = (
        jnp.einsum("thd,shd->hts", query2, all_keys, preferred_element_type=jnp.float32)
        * score_scale
    )
    allowed = jnp.concatenate([jnp.full((tok_rows, tok_rows), own_index > 0), causal], axis=1)
    logits = jnp.where(allowed[None], logits, -1e30)
    top = jnp.max(logits, axis=2, keepdims=True)
    expo = jnp.where(allowed[None], jnp.exp(logits - top), 0.0)
    weights = (expo / jnp.sum(expo, axis=2, keepdims=True)).astype(jnp.bfloat16)
    attended = jnp.einsum("hts,shd->thd", weights, all_values, preferred_element_type=jnp.float32)
    return (hidden, attended.astype(jnp.bfloat16).reshape(tok_rows, local_width))


def dot(a, b):
    return jnp.dot(a, b, preferred_element_type=F32)


def dot_nt(a, b):
    return lax.dot_general(a, b, (((1,), (1,)), ((), ())), preferred_element_type=F32)


def dot_tn(a, b):
    return lax.dot_general(a, b, (((0,), (0,)), ((), ())), preferred_element_type=F32)


def at(start, size):
    return pl.ds(pl.multiple_of(start, size), size)


ON_CHIP = pl.BlockSpec(memory_space=pltpu.VMEM)
IN_HBM = pl.BlockSpec(memory_space=pltpu.HBM)
ANYWHERE = pl.BlockSpec(memory_space=pl.ANY)


def call(body, ins, outs, in_specs=None, scratch=(), vmem=20, flops=0, moved=0):
    return pl.pallas_call(
        body,
        in_specs=in_specs or [ON_CHIP] * len(ins),
        out_specs=jax.tree.map(lambda _: ON_CHIP, outs),
        out_shape=outs,
        scratch_shapes=scratch,
        compiler_params=pltpu.CompilerParams(vmem_limit_bytes=vmem * 2**20),
        cost_estimate=pl.CostEstimate(flops=flops, bytes_accessed=moved, transcendentals=0),
    )(*ins)


def load_body(source, after, target, sems):
    rows = source.shape[-2] // sems.shape[1]
    copies = []
    for plane in range(sems.shape[0]):
        for i in range(sems.shape[1]):
            piece = (plane, pl.ds(i * rows, rows)) if len(source.shape) == 3 else pl.ds(i * rows, rows)
            copy = pltpu.make_async_copy(source.at[piece], target.at[piece], sems.at[plane, i])
            copy.start()
            copies.append(copy)
    for copy in copies:
        copy.wait()


def in_hbm(array):
    return pltpu.with_memory_space_constraint(array, pltpu.HBM)


def in_vmem(array):
    return pltpu.with_memory_space_constraint(array, pltpu.VMEM)


def loaded(array, after):
    planes = array.shape[0] if array.ndim == 3 else 1
    return call(
        load_body, (in_hbm(array), after), pltpu.VMEM(array.shape, array.dtype),
        [IN_HBM, ANYWHERE], (pltpu.SemaphoreType.DMA((planes, 4)),), vmem=4, moved=2 * array.size,
    )


def state_body(qkv_ref, send_ref, keep_ref, k_ref, v_ref, sems):
    core = lax.axis_index("seq") % 2
    count = send_ref.shape[0]
    wide = k_ref.shape[2]
    copies = []
    for slot in range(2):
        group = core if slot else 1 - core
        pair = []
        for plane, ref in ((1, k_ref), (2, v_ref)):
            copy = pltpu.make_async_copy(
                qkv_ref.at[plane, :, at(group * wide, wide)], ref.at[slot], sems.at[slot, plane - 1]
            )
            copy.start()
            pair.append(copy)
        copies.append(pair)
    for slot, out in ((0, send_ref), (1, keep_ref)):
        for copy in copies[slot]:
            copy.wait()
        for j in range(count):
            head = slice(j * HD, (j + 1) * HD)
            out[j] = dot_tn(k_ref[slot, :, head], v_ref[slot, :, head]).astype(BF16)


def intra_body(qkv_ref, o_ref, q_ref):
    rows = qkv_ref.shape[1]
    ahead = lax.broadcasted_iota(jnp.int32, (rows, rows), 1) > lax.broadcasted_iota(
        jnp.int32, (rows, rows), 0
    )
    q_ref[...] = qkv_ref[0]
    for h in range(qkv_ref.shape[2] // HD):
        head = slice(h * HD, (h + 1) * HD)
        scores = dot_nt(qkv_ref[0, :, head], qkv_ref[1, :, head])
        inner = jnp.where(ahead, 0.0, scores).astype(BF16)
        o_ref[:, head] = dot(inner, qkv_ref[2, :, head])


def quarters():
    z = lax.axis_index("head")
    edge = (z == 0) | (z == 3)
    outer, inner = (0, 3), (1, 2)
    mine = [jnp.where(edge, a, b) for a, b in zip(outer, inner)]
    other = [jnp.where(edge, b, a) for a, b in zip(outer, inner)]
    return z, mine, other


def send_body(scale, q_ref, intra_ref, own_ref, other_ref, w_ref, lin_ref, a_ref, b_ref):
    core = lax.axis_index("seq") % 2
    count = own_ref.shape[0]
    for ref, group in ((own_ref, core), (other_ref, 1 - core)):
        for j in range(count):
            head = at((group * count + j) * HD, HD)
            total = intra_ref[:, head] + dot(q_ref[:, head], ref[j])
            lin_ref[:, head] = (total * scale).astype(BF16)
    _, _, other = quarters()
    half, width = a_ref.shape[0], a_ref.shape[1] // 2
    block = width // 2
    for p in range(2):
        for n in range(2):
            product = dot(lin_ref[...], w_ref[:, at(other[p] * width + n * block, block)]).astype(BF16)
            to = slice(p * width + n * block, p * width + (n + 1) * block)
            a_ref[:, to] = product[:half]
            b_ref[:, to] = product[half:]


def mine_body(lin_ref, w_ref, r_ref, a_ref, b_ref):
    z, mine, _ = quarters()
    half, width = a_ref.shape[0], a_ref.shape[1] // 2
    block = width // 2
    for p in range(2):
        for n in range(2):
            product = dot(lin_ref[...], w_ref[:, at(mine[p] * width + n * block, block)])
            own = r_ref[:, n * block : (n + 1) * block].astype(F32)
            product = (product + jnp.where(mine[p] == z, own, 0.0)).astype(BF16)
            to = slice(p * width + n * block, p * width + (n + 1) * block)
            a_ref[:, to] = product[:half]
            b_ref[:, to] = product[half:]


def two_quarters(x_ref, w_ref, plane, which, to):
    width = x_ref.shape[1] // 2
    low = dot(x_ref[:, :width], w_ref[plane, at(which[0] * width, width), to])
    return low + dot(x_ref[:, width:], w_ref[plane, at(which[1] * width, width), to])


def first_body(block, x_ref, w_ref, acc_ref):
    _, mine, _ = quarters()
    for plane in range(3):
        for n in range(acc_ref.shape[2] // block):
            to = slice(n * block, (n + 1) * block)
            acc_ref[plane, :, to] = two_quarters(x_ref, w_ref, plane, mine, to)


def first_hidden_body(block, x_ref, w_ref, a_ref, acc_ref, hidden_ref):
    half, width = a_ref.shape[0], a_ref.shape[1] // 2
    own = at((lax.axis_index("head") // 2) * width, width)
    hidden_ref[:half] = a_ref[:, own]
    hidden_ref[half:] = x_ref[:, own]
    first_body(block, x_ref, w_ref, acc_ref)


def finish(block, plane, x_ref, w_ref, acc_ref, inv, cos, sin, out_ref):
    _, _, other = quarters()
    for n in range(acc_ref.shape[2] // block):
        to = slice(n * block, (n + 1) * block)
        total = (acc_ref[plane, :, to] + two_quarters(x_ref, w_ref, plane, other, to)) * inv
        if plane == 2:
            out_ref[:, to] = total.astype(BF16)
            continue
        for h in range(block // HD):
            value = total[:, h * HD : (h + 1) * HD]
            turned = value * cos + pltpu.roll(value, HD // 2, 1) * sin
            out_ref[:, n * block + h * HD : n * block + (h + 1) * HD] = turned.astype(BF16)


def kv_body(block, t_ref, x_ref, w_ref, acc_ref, cos_ref, sin_ref, kv_ref, inv_ref):
    t = t_ref[...].astype(F32)
    x = x_ref[...].astype(F32)
    total = jnp.sum(t * t + x * x, axis=1, keepdims=True)
    inv = lax.rsqrt(total / D + 1e-05)
    inv_ref[...] = jnp.broadcast_to(inv, inv_ref.shape)
    for plane in (1, 2):
        finish(block, plane, x_ref, w_ref, acc_ref, inv, cos_ref[...], sin_ref[...], kv_ref.at[plane - 1])


def q_body(block, x_ref, w_ref, acc_ref, inv_ref, cos_ref, sin_ref, q_ref):
    inv = inv_ref[:, :1]
    finish(block, 0, x_ref, w_ref, acc_ref, inv, cos_ref[...], sin_ref[...], q_ref)


SCORE = 1.0 / math.sqrt(HD)


def early_body(qa_ref, qb_ref, a_ref, b_ref, pa_ref, acc_ref, top_ref, sum_ref):
    has_prev = lax.axis_index("seq") > 0
    half = qa_ref.shape[0]
    shape = (2 * half, 3 * half)
    row = lax.broadcasted_iota(jnp.int32, shape, 0)
    col = lax.broadcasted_iota(jnp.int32, shape, 1)
    allowed = ((col < half) & has_prev) | ((col >= half) & (col - half <= row))
    for h in range(qa_ref.shape[1] // HD):
        head = slice(h * HD, (h + 1) * HD)
        queries = jnp.concatenate([qa_ref[:, head], qb_ref[:, head]], axis=0)
        keys = jnp.concatenate([r[0, :, head] for r in (pa_ref, a_ref, b_ref)], axis=0)
        values = jnp.concatenate([r[1, :, head] for r in (pa_ref, a_ref, b_ref)], axis=0)
        logits = jnp.where(allowed, dot_nt(queries, keys) * SCORE, NEG)
        top = jnp.max(logits, axis=1, keepdims=True)
        expo = jnp.where(allowed, jnp.exp(logits - top), 0.0)
        top_ref[h] = top
        sum_ref[h] = jnp.sum(expo, axis=1, keepdims=True)
        acc_ref[:, head] = dot(expo.astype(BF16), values)


def late_body(qa_ref, qb_ref, pb_ref, acc_ref, top_ref, sum_ref, out_ref):
    has_prev = lax.axis_index("seq") > 0
    for h in range(qa_ref.shape[1] // HD):
        head = slice(h * HD, (h + 1) * HD)
        queries = jnp.concatenate([qa_ref[:, head], qb_ref[:, head]], axis=0)
        logits = jnp.where(has_prev, dot_nt(queries, pb_ref[0, :, head]) * SCORE, NEG)
        before = top_ref[h]
        top = jnp.maximum(before, jnp.max(logits, axis=1, keepdims=True))
        expo = jnp.where(has_prev, jnp.exp(logits - top), 0.0)
        fade = jnp.exp(before - top)
        total = sum_ref[h] * fade + jnp.sum(expo, axis=1, keepdims=True)
        acc = acc_ref[:, head] * fade + dot(expo.astype(BF16), pb_ref[1, :, head])
        out_ref[:, head] = (acc / total).astype(BF16)


def tuned(lin_qkv, resid, w_out, w_qkv):
    rows, _, width = lin_qkv.shape
    nheads = width // HD
    half = rows // 2
    group = nheads // 2
    full = w_out.shape[1]
    block = width // 2
    seq = lax.axis_index("seq")
    core = seq % 2
    shape = jax.ShapeDtypeStruct

    qkv = jnp.transpose(lin_qkv, (1, 0, 2))
    wqkv = jnp.transpose(w_qkv, (1, 0, 2))

    with jax.named_scope("state"):
        states = shape((group, HD, HD), BF16)
        send, keep = call(
            state_body, (in_hbm(qkv),), (states, states), [IN_HBM],
            (
                pltpu.VMEM((2, rows, width // 2), BF16),
                pltpu.VMEM((2, rows, width // 2), BF16),
                pltpu.SemaphoreType.DMA((2, 2)),
            ),
            flops=2 * rows * width * HD, moved=4 * rows * width,
        )
        other = swapped(send, "seq", 1)
        chip_total = (keep.astype(F32) + other.astype(F32)).astype(BF16)
        by_x = swapped(chip_total, "seq", 2)
        by_y = swapped(chip_total, "seq", 4)
        by_xy = swapped(chip_total, "seq", 6)
    with jax.named_scope("intra"):
        intra, q = call(
            intra_body, (qkv,), (shape((rows, width), F32), shape((rows, width), BF16)),
            flops=4 * rows * rows * width, moved=10 * rows * width,
        )
    with jax.named_scope("load_w_out"):
        w_out_here = in_vmem(loaded(w_out, chip_total))
    with jax.named_scope("prefix"):
        x_bit = ((seq // 2) % 2).astype(F32)
        y_bit = (seq // 4).astype(F32)
        chips = (
            by_x.astype(F32) * x_bit + by_y.astype(F32) * y_bit + by_xy.astype(F32) * y_bit
        )
        low = chips.astype(BF16)
        first_core = jnp.where(core == 0, keep, other)
        high = (chips + first_core.astype(F32)).astype(BF16)
        own_prefix = jnp.where(core == 0, low, high)
        other_prefix = swapped(jnp.where(core == 0, high, low), "seq", 1)

    scale = 1.0 / math.sqrt(HD * rows * lax.axis_size("seq"))
    halves = shape((half, full // 2), BF16)
    with jax.named_scope("partials"):
        lin_out, send_a, send_b = call(
            functools.partial(send_body, scale), (q, intra, own_prefix, other_prefix, w_out_here),
            (shape((rows, width), BF16), halves, halves), flops=rows * width * full, moved=width * full,
        )
        got_a = lax.ppermute(send_a, "head", PAIR)
        mine_a, mine_b = call(
            mine_body, (lin_out, w_out_here, resid), (halves, halves),
            flops=rows * width * full, moved=width * full,
        )
    with jax.named_scope("load_w_qkv"):
        w_here = in_vmem(loaded(wqkv, mine_a))

    positions = seq * rows + jnp.arange(rows, dtype=jnp.int32)
    freq = 500000.0 ** (-(jnp.arange(HD // 2, dtype=F32) * 2.0 / HD))
    angle = positions.astype(F32)[:, None] * freq[None, :]
    cosine, sine = jnp.cos(angle), jnp.sin(angle)
    cos2 = jnp.concatenate([cosine, cosine], axis=1)
    sin2 = jnp.concatenate([-sine, sine], axis=1)

    accs = shape((3, half, width), F32)
    cost = dict(flops=half * full * 3 * width, moved=3 * width * full)

    def add(a, b):
        return (a.astype(F32) + b.astype(F32)).astype(BF16)

    def project(total, got, acc, index):
        turn = (cos2[index * half : (index + 1) * half], sin2[index * half : (index + 1) * half])
        kv, inv = call(
            functools.partial(kv_body, block), (total, got, w_here, acc, *turn),
            (shape((2, half, width), BF16), shape((half, HD), F32)), **cost,
        )
        before = shifted(kv, "seq", 1)
        query = call(
            functools.partial(q_body, block), (got, w_here, acc, inv, *turn), shape((half, width), BF16), **cost,
        )
        return kv, before, query

    with jax.named_scope("mix"):
        send_b, got_a = lax.optimization_barrier((send_b, got_a))
        got_b = lax.ppermute(send_b, "head", PAIR)
        sum_a = add(mine_a, got_a)
        far_a = lax.ppermute(sum_a, "head", CROSS)
        sum_b = add(mine_b, got_b)
        sum_b, far_a = lax.optimization_barrier((sum_b, far_a))
        far_b = lax.ppermute(sum_b, "head", CROSS)
        total_a = add(sum_a, far_a)
        rest_a = lax.ppermute(total_a, "head", PAIR)
        total_b = add(sum_b, far_b)
        rest_b = lax.ppermute(total_b, "head", PAIR)
    with jax.named_scope("project_a"):
        acc_a = call(functools.partial(first_body, block), (total_a, w_here), accs, **cost)
        kv_a, prev_a, query_a = project(total_a, rest_a, acc_a, 0)
    with jax.named_scope("project_b"):
        acc_b, hidden = call(
            functools.partial(first_hidden_body, block), (total_b, w_here, total_a),
            (accs, shape((rows, width), BF16)), **cost,
        )
        kv_b, prev_b, query_b = project(total_b, rest_b, acc_b, 1)
    with jax.named_scope("attend"):
        stat = shape((nheads, rows, 1), F32)
        acc, top, total = call(
            early_body, (query_a, query_b, kv_a, kv_b, prev_a), (shape((rows, width), F32), stat, stat),
            flops=6 * rows * rows * width, moved=12 * rows * width,
        )
        attended = call(
            late_body, (query_a, query_b, prev_b, acc, top, total), shape((rows, width), BF16),
            flops=2 * rows * rows * width, moved=12 * rows * width,
        )
    return hidden, attended


def solution(mesh):
    line = mesh.shape["seq"] == 8 and mesh.shape["head"] == 4
    return jax.shard_map(
        tuned if line else general,
        mesh=mesh,
        in_specs=(P("seq", None, "head"), P("seq", "head"), P("head", None), P(None, None, "head")),
        out_specs=(P("seq", "head"), P("seq", "head")),
        check_vma=False,
    )
```

```python
import functools
import math

import jax
import jax.numpy as jnp
from jax import lax
from jax.experimental import pallas as pl
from jax.experimental.pallas import tpu as pltpu
from jax.sharding import PartitionSpec as P

D = 4096
HD = 128
BF16 = jnp.bfloat16
F32 = jnp.float32
NEG = -1e30

PAIR = [(0, 1), (1, 0), (2, 3), (3, 2)]
CROSS = [(0, 3), (3, 0), (1, 2), (2, 1)]


def shifted(array, axis, by):
    devices = lax.axis_size(axis)
    pairs = [(i, i + by) for i in range(devices) if 0 <= i + by < devices]
    return lax.ppermute(array, axis, pairs)


def swapped(array, axis, bits):
    return lax.ppermute(array, axis, [(i, i ^ bits) for i in range(lax.axis_size(axis))])


def rotary(values, positions):
    half = values.shape[-1] // 2
    freq = 500000.0 ** (-(jnp.arange(half, dtype=jnp.float32) * 2.0 / values.shape[-1]))
    angle = positions.astype(jnp.float32)[:, None] * freq[None, :]
    cosine = jnp.cos(angle)[:, None, :]
    sine = jnp.sin(angle)[:, None, :]
    first = values[..., :half]
    second = values[..., half:]
    return jnp.concatenate(
        [first * cosine - second * sine, second * cosine + first * sine], axis=-1
    )


def general(lin_qkv, resid, w_out, w_qkv):
    tok_rows = lin_qkv.shape[0]
    local_width = lin_qkv.shape[2]
    nheads = local_width // HD
    n_seq = lax.axis_size("seq")
    own_index = lax.axis_index("seq")
    queries = lin_qkv[:, 0].reshape(tok_rows, nheads, HD)
    keys = lin_qkv[:, 1].reshape(tok_rows, nheads, HD)
    values = lin_qkv[:, 2].reshape(tok_rows, nheads, HD)
    own_state = jnp.einsum("thd,the->hde", keys, values, preferred_element_type=jnp.float32)
    piece = lax.all_gather(own_state[None], "seq", axis=0, tiled=True)
    keep = (jnp.arange(piece.shape[0], dtype=jnp.int32) < own_index).astype(jnp.float32)
    before = jnp.sum(piece * keep[:, None, None, None], axis=0)
    before = before.astype(jnp.bfloat16)
    causal = jnp.tril(jnp.ones((tok_rows, tok_rows), dtype=bool))
    scores = jnp.einsum("thd,shd->hts", queries, keys, preferred_element_type=jnp.float32)
    inner = jnp.where(causal[None], scores, 0.0).astype(jnp.bfloat16)
    total = jnp.einsum("hts,shd->thd", inner, values, preferred_element_type=jnp.float32)
    total = total + jnp.einsum("thd,hde->the", queries, before, preferred_element_type=jnp.float32)
    scale = 1.0 / math.sqrt(HD * tok_rows * n_seq)
    lin_out = (total * scale).astype(jnp.bfloat16).reshape(tok_rows, local_width)
    shared = lax.psum_scatter(
        lax.dot_general(
            w_out, lin_out, (((0,), (1,)), ((), ())), preferred_element_type=jnp.float32
        ).astype(jnp.bfloat16),
        "head",
        scatter_dimension=0,
        tiled=True,
    ).astype(jnp.float32)
    mixed_f = resid.astype(jnp.float32) + shared.T
    hidden = mixed_f.astype(jnp.bfloat16)
    flat_w = w_qkv.reshape(w_qkv.shape[0], 3 * local_width)
    squared = lax.psum(jnp.sum(mixed_f * mixed_f, axis=1), "head")
    normed = (mixed_f * lax.rsqrt(squared[:, None] / D + 1e-05)).astype(jnp.bfloat16)
    proj = jnp.dot(
        lax.all_gather(normed, "head", axis=1, tiled=True),
        flat_w,
        preferred_element_type=jnp.float32,
    )
    proj = proj.reshape(tok_rows, 3, nheads, HD)
    positions = own_index * tok_rows + jnp.arange(tok_rows, dtype=jnp.int32)
    query2 = rotary(proj[:, 0], positions).astype(jnp.bfloat16)
    key2 = rotary(proj[:, 1], positions).astype(jnp.bfloat16)
    value2 = proj[:, 2].astype(jnp.bfloat16)
    key_prev, value_prev = shifted((key2, value2), "seq", 1)
    score_scale = 1.0 / math.sqrt(HD)
    all_keys = jnp.concatenate([key_prev, key2], axis=0)
    all_values = jnp.concatenate([value_prev, value2], axis=0)
    logits = (
        jnp.einsum("thd,shd->hts", query2, all_keys, preferred_element_type=jnp.float32)
        * score_scale
    )
    allowed = jnp.concatenate([jnp.full((tok_rows, tok_rows), own_index > 0), causal], axis=1)
    logits = jnp.where(allowed[None], logits, -1e30)
    top = jnp.max(logits, axis=2, keepdims=True)
    expo = jnp.where(allowed[None], jnp.exp(logits - top), 0.0)
    weights = (expo / jnp.sum(expo, axis=2, keepdims=True)).astype(jnp.bfloat16)
    attended = jnp.einsum("hts,shd->thd", weights, all_values, preferred_element_type=jnp.float32)
    return (hidden, attended.astype(jnp.bfloat16).reshape(tok_rows, local_width))


def dot(a, b):
    return jnp.dot(a, b, preferred_element_type=F32)


def dot_nt(a, b):
    return lax.dot_general(a, b, (((1,), (1,)), ((), ())), preferred_element_type=F32)


def dot_tn(a, b):
    return lax.dot_general(a, b, (((0,), (0,)), ((), ())), preferred_element_type=F32)


def at(start, size):
    return pl.ds(pl.multiple_of(start, size), size)


ON_CHIP = pl.BlockSpec(memory_space=pltpu.VMEM)
IN_HBM = pl.BlockSpec(memory_space=pltpu.HBM)
ANYWHERE = pl.BlockSpec(memory_space=pl.ANY)


def call(body, ins, outs, in_specs=None, scratch=(), vmem=8, flops=0, moved=0):
    return pl.pallas_call(
        body,
        in_specs=in_specs or [ON_CHIP] * len(ins),
        out_specs=jax.tree.map(lambda _: ON_CHIP, outs),
        out_shape=outs,
        scratch_shapes=scratch,
        compiler_params=pltpu.CompilerParams(vmem_limit_bytes=vmem * 2**20),
        cost_estimate=pl.CostEstimate(flops=flops, bytes_accessed=moved, transcendentals=0),
    )(*ins)


def start_all(pairs, sems):
    copies = [pltpu.make_async_copy(a, b, sems.at[i]) for i, (a, b) in enumerate(pairs)]
    for copy in copies:
        copy.start()
    return copies


def in_hbm(array):
    return pltpu.with_memory_space_constraint(array, pltpu.HBM)


def in_vmem(array):
    return pltpu.with_memory_space_constraint(array, pltpu.VMEM)


def state_body(qkv_ref, send_ref, keep_ref, k_ref, v_ref, sems):
    core = lax.axis_index("seq") % 2
    count = send_ref.shape[0]
    wide = k_ref.shape[2]
    copies = []
    for slot in range(2):
        group = core if slot else 1 - core
        pair = []
        for plane, ref in ((1, k_ref), (2, v_ref)):
            copy = pltpu.make_async_copy(
                qkv_ref.at[plane, :, at(group * wide, wide)], ref.at[slot], sems.at[slot, plane - 1]
            )
            copy.start()
            pair.append(copy)
        copies.append(pair)
    for slot, out in ((0, send_ref), (1, keep_ref)):
        for copy in copies[slot]:
            copy.wait()
        for j in range(count):
            head = slice(j * HD, (j + 1) * HD)
            out[j] = dot_tn(k_ref[slot, :, head], v_ref[slot, :, head]).astype(BF16)


def intra_body(qkv_ref, after, cos_ref, sin_ref, w_ref, o_ref, q_ref, w_other_ref, w_mine_ref, sems):
    _, mine, other = quarters()
    width = w_mine_ref.shape[2]
    copies = start_all(
        [
            (w_ref.at[:, at(which[p] * width, width)], to.at[p])
            for which, to in ((other, w_other_ref), (mine, w_mine_ref))
            for p in range(2)
        ],
        sems,
    )
    rows = qkv_ref.shape[1]
    ahead = lax.broadcasted_iota(jnp.int32, (rows, rows), 1) > lax.broadcasted_iota(
        jnp.int32, (rows, rows), 0
    )
    q_ref[...] = qkv_ref[0]
    for h in range(qkv_ref.shape[2] // HD):
        head = slice(h * HD, (h + 1) * HD)
        scores = dot_nt(qkv_ref[0, :, head], qkv_ref[1, :, head])
        inner = jnp.where(ahead, 0.0, scores).astype(BF16)
        o_ref[:, head] = dot(inner, qkv_ref[2, :, head])
    for copy in copies:
        copy.wait()


def quarters():
    z = lax.axis_index("head")
    edge = (z == 0) | (z == 3)
    outer, inner = (0, 3), (1, 2)
    mine = [jnp.where(edge, a, b) for a, b in zip(outer, inner)]
    other = [jnp.where(edge, b, a) for a, b in zip(outer, inner)]
    return z, mine, other


def send_body(scale, q_ref, intra_ref, own_ref, other_ref, w_ref, lin_ref, a_ref, b_ref):
    core = lax.axis_index("seq") % 2
    count = own_ref.shape[0]
    for ref, group in ((own_ref, core), (other_ref, 1 - core)):
        for j in range(count):
            head = at((group * count + j) * HD, HD)
            total = intra_ref[:, head] + dot(q_ref[:, head], ref[j])
            lin_ref[:, head] = (total * scale).astype(BF16)
    half, width = a_ref.shape[0], a_ref.shape[1] // 2
    block = width // 2
    for p in range(2):
        for n in range(2):
            product = dot(lin_ref[...], w_ref[p, :, n * block : (n + 1) * block]).astype(BF16)
            to = slice(p * width + n * block, p * width + (n + 1) * block)
            a_ref[:, to] = product[:half]
            b_ref[:, to] = product[half:]


def mine_body(lin_ref, w_ref, r_ref, w_qkv_ref, a_ref, b_ref, w_qkv_to_ref, sems):
    z, mine, _ = quarters()
    copies = start_all(
        [
            (w_qkv_ref.at[j, pl.ds(i, r_ref.shape[1])], w_qkv_to_ref.at[j, pl.ds(i, r_ref.shape[1])])
            for j in range(3)
            for i in range(0, w_qkv_ref.shape[1], r_ref.shape[1])
        ],
        sems,
    )
    half, width = a_ref.shape[0], a_ref.shape[1] // 2
    block = width // 2
    for p in range(2):
        for n in range(2):
            product = dot(lin_ref[...], w_ref[p, :, n * block : (n + 1) * block])
            own = r_ref[:, n * block : (n + 1) * block].astype(F32)
            product = (product + jnp.where(mine[p] == z, own, 0.0)).astype(BF16)
            to = slice(p * width + n * block, p * width + (n + 1) * block)
            a_ref[:, to] = product[:half]
            b_ref[:, to] = product[half:]
    for copy in copies:
        copy.wait()


def add_body(a_ref, b_ref, o_ref):
    o_ref[...] = (a_ref[...].astype(F32) + b_ref[...].astype(F32)).astype(BF16)


def two_quarters(x_ref, w_ref, plane, which, to):
    width = x_ref.shape[1] // 2
    low = dot(x_ref[:, :width], w_ref[plane, at(which[0] * width, width), to])
    return low + dot(x_ref[:, width:], w_ref[plane, at(which[1] * width, width), to])


def first_body(block, x_ref, w_ref, acc_ref):
    _, mine, _ = quarters()
    for plane in range(3):
        for n in range(acc_ref.shape[2] // block):
            to = slice(n * block, (n + 1) * block)
            acc_ref[plane, :, to] = two_quarters(x_ref, w_ref, plane, mine, to)


def first_hidden_body(block, x_ref, w_ref, a_ref, acc_ref, hidden_ref):
    half, width = a_ref.shape[0], a_ref.shape[1] // 2
    own = at((lax.axis_index("head") // 2) * width, width)
    hidden_ref[:half] = a_ref[:, own]
    hidden_ref[half:] = x_ref[:, own]
    first_body(block, x_ref, w_ref, acc_ref)


def finish(block, plane, x_ref, w_ref, acc_ref, inv, cos, sin, out_ref):
    _, _, other = quarters()
    for n in range(acc_ref.shape[2] // block):
        to = slice(n * block, (n + 1) * block)
        total = (acc_ref[plane, :, to] + two_quarters(x_ref, w_ref, plane, other, to)) * inv
        if plane == 2:
            out_ref[:, to] = total.astype(BF16)
            continue
        for h in range(block // HD):
            value = total[:, h * HD : (h + 1) * HD]
            turned = value * cos + pltpu.roll(value, HD // 2, 1) * sin
            out_ref[:, n * block + h * HD : n * block + (h + 1) * HD] = turned.astype(BF16)


def kv_body(block, mine, t_ref, x_ref, w_ref, acc_ref, cos_ref, sin_ref, kv_ref, inv_ref):
    t = t_ref[...].astype(F32)
    x = x_ref[...].astype(F32)
    total = jnp.sum(t * t + x * x, axis=1, keepdims=True)
    inv = lax.rsqrt(total / D + 1e-05)
    inv_ref[...] = jnp.broadcast_to(inv, inv_ref.shape)
    for plane in (1, 2):
        finish(block, plane, x_ref, w_ref, acc_ref, inv, cos_ref[mine], sin_ref[mine], kv_ref.at[plane - 1])


def q_body(block, mine, x_ref, w_ref, acc_ref, inv_ref, cos_ref, sin_ref, q_ref):
    inv = inv_ref[:, :1]
    finish(block, 0, x_ref, w_ref, acc_ref, inv, cos_ref[mine], sin_ref[mine], q_ref)


SCORE = 1.0 / math.sqrt(HD)


def early_body(qa_ref, qb_ref, a_ref, b_ref, pa_ref, acc_ref, top_ref, sum_ref):
    has_prev = lax.axis_index("seq") > 0
    half = qa_ref.shape[0]
    shape = (2 * half, 3 * half)
    row = lax.broadcasted_iota(jnp.int32, shape, 0)
    col = lax.broadcasted_iota(jnp.int32, shape, 1)
    allowed = ((col < half) & has_prev) | ((col >= half) & (col - half <= row))
    for h in range(qa_ref.shape[1] // HD):
        head = slice(h * HD, (h + 1) * HD)
        queries = jnp.concatenate([qa_ref[:, head], qb_ref[:, head]], axis=0)
        keys = jnp.concatenate([r[0, :, head] for r in (pa_ref, a_ref, b_ref)], axis=0)
        values = jnp.concatenate([r[1, :, head] for r in (pa_ref, a_ref, b_ref)], axis=0)
        logits = jnp.where(allowed, dot_nt(queries, keys) * SCORE, NEG)
        top = jnp.max(logits, axis=1, keepdims=True)
        expo = jnp.where(allowed, jnp.exp(logits - top), 0.0)
        top_ref[h] = top
        sum_ref[h] = jnp.sum(expo, axis=1, keepdims=True)
        acc_ref[:, head] = dot(expo.astype(BF16), values)


def late_body(qa_ref, qb_ref, pb_ref, acc_ref, top_ref, sum_ref, out_ref):
    has_prev = lax.axis_index("seq") > 0
    for h in range(qa_ref.shape[1] // HD):
        head = slice(h * HD, (h + 1) * HD)
        queries = jnp.concatenate([qa_ref[:, head], qb_ref[:, head]], axis=0)
        logits = jnp.where(has_prev, dot_nt(queries, pb_ref[0, :, head]) * SCORE, NEG)
        before = top_ref[h]
        top = jnp.maximum(before, jnp.max(logits, axis=1, keepdims=True))
        expo = jnp.where(has_prev, jnp.exp(logits - top), 0.0)
        fade = jnp.exp(before - top)
        total = sum_ref[h] * fade + jnp.sum(expo, axis=1, keepdims=True)
        acc = acc_ref[:, head] * fade + dot(expo.astype(BF16), pb_ref[1, :, head])
        out_ref[:, head] = (acc / total).astype(BF16)


def tuned(lin_qkv, resid, w_out, w_qkv):
    rows, _, width = lin_qkv.shape
    nheads = width // HD
    half = rows // 2
    group = nheads // 2
    full = w_out.shape[1]
    block = width // 2
    seq = lax.axis_index("seq")
    core = seq % 2
    shape = jax.ShapeDtypeStruct

    qkv = jnp.transpose(lin_qkv, (1, 0, 2))
    wqkv = jnp.transpose(w_qkv, (1, 0, 2))

    positions = seq * rows + jnp.arange(rows, dtype=jnp.int32)
    freq = 500000.0 ** (-(jnp.arange(HD // 2, dtype=F32) * 2.0 / HD))
    angle = positions.astype(F32)[:, None] * freq[None, :]
    cosine, sine = jnp.cos(angle), jnp.sin(angle)
    cos2 = jnp.concatenate([cosine, cosine], axis=1)
    sin2 = jnp.concatenate([-sine, sine], axis=1)

    with jax.named_scope("state"):
        states = shape((group, HD, HD), BF16)
        send, keep = call(
            state_body, (in_hbm(qkv),), (states, states), [IN_HBM],
            (
                pltpu.VMEM((2, rows, width // 2), BF16),
                pltpu.VMEM((2, rows, width // 2), BF16),
                pltpu.SemaphoreType.DMA((2, 2)),
            ),
            flops=2 * rows * width * HD, moved=4 * rows * width,
        )
        other = swapped(send, "seq", 1)
        chip_total = (keep.astype(F32) + other.astype(F32)).astype(BF16)
        by_x = swapped(chip_total, "seq", 2)
        by_y = swapped(chip_total, "seq", 4)
        by_xy = swapped(chip_total, "seq", 6)
    with jax.named_scope("intra"):
        columns = pltpu.VMEM((2, width, width), BF16)
        intra, q, w_other, w_mine = call(
            intra_body, (qkv, chip_total, cos2, sin2, in_hbm(w_out)),
            (shape((rows, width), F32), shape((rows, width), BF16), columns, columns),
            [ON_CHIP, ANYWHERE, ANYWHERE, ANYWHERE, IN_HBM], (pltpu.SemaphoreType.DMA((4,)),),
            flops=4 * rows * rows * width, moved=2 * width * full,
        )
    with jax.named_scope("prefix"):
        x_bit = ((seq // 2) % 2).astype(F32)
        y_bit = (seq // 4).astype(F32)
        chips = (
            by_x.astype(F32) * x_bit + by_y.astype(F32) * y_bit + by_xy.astype(F32) * y_bit
        )
        low = chips.astype(BF16)
        first_core = jnp.where(core == 0, keep, other)
        high = (chips + first_core.astype(F32)).astype(BF16)
        own_prefix = jnp.where(core == 0, low, high)
        other_prefix = swapped(jnp.where(core == 0, high, low), "seq", 1)

    scale = 1.0 / math.sqrt(HD * rows * lax.axis_size("seq"))
    halves = shape((half, full // 2), BF16)
    with jax.named_scope("partials"):
        lin_out, send_a, send_b = call(
            functools.partial(send_body, scale), (q, intra, own_prefix, other_prefix, in_vmem(w_other)),
            (shape((rows, width), BF16), halves, halves), flops=rows * width * full, moved=width * full,
        )
        got_a = lax.ppermute(send_a, "head", PAIR)
        mine_a, mine_b, w_here = call(
            mine_body, (lin_out, in_vmem(w_mine), resid, in_hbm(wqkv)),
            (halves, halves, pltpu.VMEM(wqkv.shape, BF16)),
            [ON_CHIP, ON_CHIP, ON_CHIP, IN_HBM], (pltpu.SemaphoreType.DMA((3 * full // width,)),),
            flops=rows * width * full, moved=6 * width * full,
        )
        w_here = in_vmem(w_here)
    accs = shape((3, half, width), F32)
    cost = dict(flops=half * full * 3 * width, moved=3 * width * full)

    def add(a, b):
        return call(add_body, (a, b), halves, vmem=4, moved=6 * half * full)

    def project(total, got, acc, index):
        turn = (cos2, sin2)
        mine = pl.ds(index * half, half)
        kv, inv = call(
            functools.partial(kv_body, block, mine), (total, got, w_here, acc, *turn),
            (shape((2, half, width), BF16), shape((half, HD), F32)), **cost,
        )
        before = shifted(kv, "seq", 1)
        query = call(
            functools.partial(q_body, block, mine), (got, w_here, acc, inv, *turn), shape((half, width), BF16), **cost,
        )
        return kv, before, query

    with jax.named_scope("mix"):
        send_b, got_a = lax.optimization_barrier((send_b, got_a))
        got_b = lax.ppermute(send_b, "head", PAIR)
        sum_a = add(mine_a, got_a)
        far_a = lax.ppermute(sum_a, "head", CROSS)
        sum_b = add(mine_b, got_b)
        sum_b, far_a = lax.optimization_barrier((sum_b, far_a))
        far_b = lax.ppermute(sum_b, "head", CROSS)
        total_a = add(sum_a, far_a)
        rest_a = lax.ppermute(total_a, "head", PAIR)
        total_b = add(sum_b, far_b)
        rest_b = lax.ppermute(total_b, "head", PAIR)
    with jax.named_scope("project_a"):
        acc_a = call(functools.partial(first_body, block), (total_a, w_here), accs, **cost)
        kv_a, prev_a, query_a = project(total_a, rest_a, acc_a, 0)
    with jax.named_scope("project_b"):
        acc_b, hidden = call(
            functools.partial(first_hidden_body, block), (total_b, w_here, total_a),
            (accs, shape((rows, width), BF16)), **cost,
        )
        kv_b, prev_b, query_b = project(total_b, rest_b, acc_b, 1)
    with jax.named_scope("attend"):
        stat = shape((nheads, rows, 1), F32)
        acc, top, total = call(
            early_body, (query_a, query_b, kv_a, kv_b, prev_a), (shape((rows, width), F32), stat, stat),
            flops=6 * rows * rows * width, moved=12 * rows * width,
        )
        attended = call(
            late_body, (query_a, query_b, prev_b, acc, top, total), shape((rows, width), BF16),
            flops=2 * rows * rows * width, moved=12 * rows * width,
        )
    return hidden, attended


def solution(mesh):
    line = mesh.shape["seq"] == 8 and mesh.shape["head"] == 4
    return jax.shard_map(
        tuned if line else general,
        mesh=mesh,
        in_specs=(P("seq", None, "head"), P("seq", "head"), P("head", None), P(None, None, "head")),
        out_specs=(P("seq", "head"), P("seq", "head")),
        check_vma=False,
    )
```

```python
import functools
import math

import jax
import jax.numpy as jnp
from jax import lax
from jax.experimental import pallas as pl
from jax.experimental.pallas import tpu as pltpu
from jax.sharding import PartitionSpec as P

D = 4096
HD = 128
BF16 = jnp.bfloat16
F32 = jnp.float32
NEG = -1e30
STREAMS = (1, 1)

PAIR = [(0, 1), (1, 0), (2, 3), (3, 2)]
CROSS = [(0, 3), (3, 0), (1, 2), (2, 1)]


def shifted(array, axis, by):
    devices = lax.axis_size(axis)
    pairs = [(i, i + by) for i in range(devices) if 0 <= i + by < devices]
    return lax.ppermute(array, axis, pairs)


def swapped(array, axis, bits):
    return lax.ppermute(array, axis, [(i, i ^ bits) for i in range(lax.axis_size(axis))])


def rotary(values, positions):
    half = values.shape[-1] // 2
    freq = 500000.0 ** (-(jnp.arange(half, dtype=jnp.float32) * 2.0 / values.shape[-1]))
    angle = positions.astype(jnp.float32)[:, None] * freq[None, :]
    cosine = jnp.cos(angle)[:, None, :]
    sine = jnp.sin(angle)[:, None, :]
    first = values[..., :half]
    second = values[..., half:]
    return jnp.concatenate(
        [first * cosine - second * sine, second * cosine + first * sine], axis=-1
    )


def general(lin_qkv, resid, w_out, w_qkv):
    tok_rows = lin_qkv.shape[0]
    local_width = lin_qkv.shape[2]
    nheads = local_width // HD
    n_seq = lax.axis_size("seq")
    own_index = lax.axis_index("seq")
    queries = lin_qkv[:, 0].reshape(tok_rows, nheads, HD)
    keys = lin_qkv[:, 1].reshape(tok_rows, nheads, HD)
    values = lin_qkv[:, 2].reshape(tok_rows, nheads, HD)
    own_state = jnp.einsum("thd,the->hde", keys, values, preferred_element_type=jnp.float32)
    piece = lax.all_gather(own_state[None], "seq", axis=0, tiled=True)
    keep = (jnp.arange(piece.shape[0], dtype=jnp.int32) < own_index).astype(jnp.float32)
    before = jnp.sum(piece * keep[:, None, None, None], axis=0)
    before = before.astype(jnp.bfloat16)
    causal = jnp.tril(jnp.ones((tok_rows, tok_rows), dtype=bool))
    scores = jnp.einsum("thd,shd->hts", queries, keys, preferred_element_type=jnp.float32)
    inner = jnp.where(causal[None], scores, 0.0).astype(jnp.bfloat16)
    total = jnp.einsum("hts,shd->thd", inner, values, preferred_element_type=jnp.float32)
    total = total + jnp.einsum("thd,hde->the", queries, before, preferred_element_type=jnp.float32)
    scale = 1.0 / math.sqrt(HD * tok_rows * n_seq)
    lin_out = (total * scale).astype(jnp.bfloat16).reshape(tok_rows, local_width)
    shared = lax.psum_scatter(
        lax.dot_general(
            w_out, lin_out, (((0,), (1,)), ((), ())), preferred_element_type=jnp.float32
        ).astype(jnp.bfloat16),
        "head",
        scatter_dimension=0,
        tiled=True,
    ).astype(jnp.float32)
    mixed_f = resid.astype(jnp.float32) + shared.T
    hidden = mixed_f.astype(jnp.bfloat16)
    flat_w = w_qkv.reshape(w_qkv.shape[0], 3 * local_width)
    squared = lax.psum(jnp.sum(mixed_f * mixed_f, axis=1), "head")
    normed = (mixed_f * lax.rsqrt(squared[:, None] / D + 1e-05)).astype(jnp.bfloat16)
    proj = jnp.dot(
        lax.all_gather(normed, "head", axis=1, tiled=True),
        flat_w,
        preferred_element_type=jnp.float32,
    )
    proj = proj.reshape(tok_rows, 3, nheads, HD)
    positions = own_index * tok_rows + jnp.arange(tok_rows, dtype=jnp.int32)
    query2 = rotary(proj[:, 0], positions).astype(jnp.bfloat16)
    key2 = rotary(proj[:, 1], positions).astype(jnp.bfloat16)
    value2 = proj[:, 2].astype(jnp.bfloat16)
    key_prev, value_prev = shifted((key2, value2), "seq", 1)
    score_scale = 1.0 / math.sqrt(HD)
    all_keys = jnp.concatenate([key_prev, key2], axis=0)
    all_values = jnp.concatenate([value_prev, value2], axis=0)
    logits = (
        jnp.einsum("thd,shd->hts", query2, all_keys, preferred_element_type=jnp.float32)
        * score_scale
    )
    allowed = jnp.concatenate([jnp.full((tok_rows, tok_rows), own_index > 0), causal], axis=1)
    logits = jnp.where(allowed[None], logits, -1e30)
    top = jnp.max(logits, axis=2, keepdims=True)
    expo = jnp.where(allowed[None], jnp.exp(logits - top), 0.0)
    weights = (expo / jnp.sum(expo, axis=2, keepdims=True)).astype(jnp.bfloat16)
    attended = jnp.einsum("hts,shd->thd", weights, all_values, preferred_element_type=jnp.float32)
    return (hidden, attended.astype(jnp.bfloat16).reshape(tok_rows, local_width))


def dot(a, b):
    return jnp.dot(a, b, preferred_element_type=F32)


def dot_nt(a, b):
    return lax.dot_general(a, b, (((1,), (1,)), ((), ())), preferred_element_type=F32)


def dot_tn(a, b):
    return lax.dot_general(a, b, (((0,), (0,)), ((), ())), preferred_element_type=F32)


def at(start, size):
    return pl.ds(pl.multiple_of(start, size), size)


ON_CHIP = pl.BlockSpec(memory_space=pltpu.VMEM)
IN_HBM = pl.BlockSpec(memory_space=pltpu.HBM)
ANYWHERE = pl.BlockSpec(memory_space=pl.ANY)


def call(body, ins, outs, in_specs=None, scratch=(), vmem=8, flops=0, moved=0):
    return pl.pallas_call(
        body,
        in_specs=in_specs or [ON_CHIP] * len(ins),
        out_specs=jax.tree.map(lambda _: ON_CHIP, outs),
        out_shape=outs,
        scratch_shapes=scratch,
        compiler_params=pltpu.CompilerParams(vmem_limit_bytes=vmem * 2**20),
        cost_estimate=pl.CostEstimate(flops=flops, bytes_accessed=moved, transcendentals=0),
    )(*ins)


def start_all(pairs, sems):
    copies = [pltpu.make_async_copy(a, b, sems.at[i]) for i, (a, b) in enumerate(pairs)]
    for copy in copies:
        copy.start()
    return copies


def in_hbm(array):
    return pltpu.with_memory_space_constraint(array, pltpu.HBM)


def in_vmem(array):
    return pltpu.with_memory_space_constraint(array, pltpu.VMEM)


def state_body(qkv_ref, send_ref, keep_ref, k_ref, v_ref, sems):
    core = lax.axis_index("seq") % 2
    count = send_ref.shape[0]
    wide = k_ref.shape[2]
    copies = []
    for slot in range(2):
        group = core if slot else 1 - core
        pair = []
        for plane, ref in ((1, k_ref), (2, v_ref)):
            copy = pltpu.make_async_copy(
                qkv_ref.at[plane, :, at(group * wide, wide)], ref.at[slot], sems.at[slot, plane - 1]
            )
            copy.start()
            pair.append(copy)
        copies.append(pair)
    for slot, out in ((0, send_ref), (1, keep_ref)):
        for copy in copies[slot]:
            copy.wait()
        for j in range(count):
            head = slice(j * HD, (j + 1) * HD)
            out[j] = dot_tn(k_ref[slot, :, head], v_ref[slot, :, head]).astype(BF16)


def intra_body(qkv_ref, after, cos_ref, sin_ref, w_ref, o_ref, q_ref, w_other_ref, w_mine_ref, sems):
    _, mine, other = quarters()
    width = w_mine_ref.shape[2]
    copies = start_all(
        [
            (w_ref.at[:, at(which[p] * width, width)], to.at[p])
            for which, to in ((other, w_other_ref), (mine, w_mine_ref))
            for p in range(2)
        ],
        sems,
    )
    rows = qkv_ref.shape[1]
    ahead = lax.broadcasted_iota(jnp.int32, (rows, rows), 1) > lax.broadcasted_iota(
        jnp.int32, (rows, rows), 0
    )
    q_ref[...] = qkv_ref[0]
    for h in range(qkv_ref.shape[2] // HD):
        head = slice(h * HD, (h + 1) * HD)
        scores = dot_nt(qkv_ref[0, :, head], qkv_ref[1, :, head])
        inner = jnp.where(ahead, 0.0, scores).astype(BF16)
        o_ref[:, head] = dot(inner, qkv_ref[2, :, head])
    for copy in copies:
        copy.wait()


def quarters():
    z = lax.axis_index("head")
    edge = (z == 0) | (z == 3)
    outer, inner = (0, 3), (1, 2)
    mine = [jnp.where(edge, a, b) for a, b in zip(outer, inner)]
    other = [jnp.where(edge, b, a) for a, b in zip(outer, inner)]
    return z, mine, other


def lin_out_rows(scale, rows, q_ref, intra_ref, own_ref, other_ref, lin_ref):
    core = lax.axis_index("seq") % 2
    count = own_ref.shape[0]
    for ref, group in ((own_ref, core), (other_ref, 1 - core)):
        for j in range(count):
            head = at((group * count + j) * HD, HD)
            total = intra_ref[rows, head] + dot(q_ref[rows, head], ref[j])
            lin_ref[rows, head] = (total * scale).astype(BF16)


def send_body(scale, cuts, q_ref, intra_ref, own_ref, other_ref, w_ref, send_ref, lin_ref):
    rows = slice(*cuts[0])
    lin_out_rows(scale, rows, q_ref, intra_ref, own_ref, other_ref, lin_ref)
    width = w_ref.shape[2]
    block = width // 2
    for p in range(2):
        for n in range(2):
            to = slice(p * width + n * block, p * width + (n + 1) * block)
            send_ref[:, to] = dot(lin_ref[rows], w_ref[p, :, n * block : (n + 1) * block]).astype(BF16)


def mine_body(scale, cuts, *refs):
    q_ref, intra_ref, own_ref, other_ref, w_other_ref, w_mine_ref, r_ref, w_qkv_ref = refs[:8]
    count = len(cuts)
    send_refs, mine_refs = refs[8 : 7 + count], refs[7 + count : 7 + 2 * count]
    w_qkv_to_ref, lin_ref, sems = refs[7 + 2 * count :]
    z, mine, _ = quarters()
    width = w_mine_ref.shape[2]
    block = width // 2
    copies = start_all(
        [
            (w_qkv_ref.at[j, pl.ds(i, width)], w_qkv_to_ref.at[j, pl.ds(i, width)])
            for j in range(3)
            for i in range(0, w_qkv_ref.shape[1], width)
        ],
        sems,
    )
    lin_out_rows(scale, slice(None), q_ref, intra_ref, own_ref, other_ref, lin_ref)
    skip = cuts[0][1]
    for p in range(2):
        for n in range(2):
            part = slice(n * block, (n + 1) * block)
            to = slice(p * width + n * block, p * width + (n + 1) * block)
            product = dot(lin_ref[skip:], w_other_ref[p, :, part]).astype(BF16)
            for (a, b), ref in zip(cuts[1:], send_refs):
                ref[:, to] = product[a - skip : b - skip]
    for p in range(2):
        for n in range(2):
            part = slice(n * block, (n + 1) * block)
            to = slice(p * width + n * block, p * width + (n + 1) * block)
            product = dot(lin_ref[...], w_mine_ref[p, :, part])
            own = jnp.where(mine[p] == z, r_ref[:, part].astype(F32), 0.0)
            product = (product + own).astype(BF16)
            for (a, b), ref in zip(cuts, mine_refs):
                ref[:, to] = product[a:b]
    for copy in copies:
        copy.wait()


def add_body(a_ref, b_ref, o_ref):
    o_ref[...] = (a_ref[...].astype(F32) + b_ref[...].astype(F32)).astype(BF16)


def two_quarters(x_ref, w_ref, plane, which, to):
    width = x_ref.shape[1] // 2
    low = dot(x_ref[:, :width], w_ref[plane, at(which[0] * width, width), to])
    return low + dot(x_ref[:, width:], w_ref[plane, at(which[1] * width, width), to])


def first_body(block, x_ref, w_ref, acc_ref):
    _, mine, _ = quarters()
    for plane in range(3):
        for n in range(acc_ref.shape[2] // block):
            to = slice(n * block, (n + 1) * block)
            acc_ref[plane, :, to] = two_quarters(x_ref, w_ref, plane, mine, to)


def first_hidden_body(block, cuts, x_ref, w_ref, *refs):
    total_refs, (acc_ref, hidden_ref) = refs[:-2], refs[-2:]
    width = acc_ref.shape[2]
    own = at((lax.axis_index("head") // 2) * width, width)
    for (a, b), ref in zip(cuts, (*total_refs, x_ref)):
        hidden_ref[a:b] = ref[:, own]
    first_body(block, x_ref, w_ref, acc_ref)


def finish(block, plane, x_ref, w_ref, acc_ref, inv, cos, sin, out_ref):
    _, _, other = quarters()
    for n in range(acc_ref.shape[2] // block):
        to = slice(n * block, (n + 1) * block)
        total = (acc_ref[plane, :, to] + two_quarters(x_ref, w_ref, plane, other, to)) * inv
        if plane == 2:
            out_ref[:, to] = total.astype(BF16)
            continue
        for h in range(block // HD):
            value = total[:, h * HD : (h + 1) * HD]
            turned = value * cos + pltpu.roll(value, HD // 2, 1) * sin
            out_ref[:, n * block + h * HD : n * block + (h + 1) * HD] = turned.astype(BF16)


def kv_body(block, rows, t_ref, x_ref, w_ref, acc_ref, cos_ref, sin_ref, after, kv_ref, rest_ref):
    t = t_ref[...].astype(F32)
    x = x_ref[...].astype(F32)
    total = jnp.sum(t * t + x * x, axis=1, keepdims=True)
    inv = lax.rsqrt(total / D + 1e-05)
    cos, sin = cos_ref[slice(*rows)], sin_ref[slice(*rows)]
    for plane in (1, 2):
        finish(block, plane, x_ref, w_ref, acc_ref, inv, cos, sin, kv_ref.at[plane - 1])
    if rest_ref.dtype == BF16:
        finish(block, 0, x_ref, w_ref, acc_ref, inv, cos, sin, rest_ref)
    else:
        rest_ref[...] = jnp.broadcast_to(inv, rest_ref.shape)


SCORE = 1.0 / math.sqrt(HD)


def stacked(refs, *where):
    return jnp.concatenate([ref[where] for ref in refs], axis=0)


def early_body(block, cuts, *refs):
    count = len(cuts)
    x_ref, w_ref, acc_in_ref, inv_ref, cos_ref, sin_ref = refs[:6]
    q_refs, kv_refs = refs[6 : 5 + count], refs[5 + count : 5 + 2 * count]
    prev_refs = refs[5 + 2 * count : 4 + 3 * count]
    q_ref, acc_ref, top_ref, sum_ref = refs[4 + 3 * count :]
    rows = slice(*cuts[-1])
    finish(block, 0, x_ref, w_ref, acc_in_ref, inv_ref[:, :1], cos_ref[rows], sin_ref[rows], q_ref)
    q_refs = (*q_refs, q_ref)
    has_prev = lax.axis_index("seq") > 0
    before = cuts[-1][0]
    shape = (before + cuts[-1][1], cuts[-1][1])
    key = lax.broadcasted_iota(jnp.int32, shape, 0)
    query = lax.broadcasted_iota(jnp.int32, shape, 1)
    allowed = ((key < before) & has_prev) | ((key >= before) & (key - before <= query))
    for h in range(q_ref.shape[1] // HD):
        head = slice(h * HD, (h + 1) * HD)
        keys = stacked((*prev_refs, *kv_refs), 0, slice(None), head)
        values = stacked((*prev_refs, *kv_refs), 1, slice(None), head)
        logits = dot_nt(keys, stacked(q_refs, slice(None), head)) * SCORE
        logits = jnp.where(allowed, logits, NEG)
        top = jnp.max(logits, axis=0, keepdims=True)
        expo = jnp.where(allowed, jnp.exp(logits - top), 0.0)
        top_ref[h : h + 1] = top
        sum_ref[h : h + 1] = jnp.sum(expo, axis=0, keepdims=True)
        acc_ref[h] = dot_tn(values, expo.astype(BF16))


def late_body(count, *refs):
    q_refs, (prev_ref, acc_ref, top_ref, sum_ref, out_ref) = refs[:count], refs[count:]
    has_prev = lax.axis_index("seq") > 0
    heads = range(out_ref.shape[1] // HD)
    at_head = [slice(h * HD, (h + 1) * HD) for h in heads]
    logits = [
        jnp.where(has_prev, dot_nt(prev_ref[0, :, at], stacked(q_refs, slice(None), at)) * SCORE, NEG)
        for at in at_head
    ]
    highest = jnp.concatenate([jnp.max(x, axis=0, keepdims=True) for x in logits], axis=0)
    top = jnp.maximum(top_ref[...], highest)
    fade = jnp.exp(top_ref[...] - top)
    expo = [jnp.where(has_prev, jnp.exp(logits[h] - top[h : h + 1]), 0.0) for h in heads]
    sums = jnp.concatenate([jnp.sum(x, axis=0, keepdims=True) for x in expo], axis=0)
    inverse = 1.0 / (sum_ref[...] * fade + sums)
    fade = fade * inverse
    for h in heads:
        weights = (expo[h] * inverse[h : h + 1]).astype(BF16)
        total = acc_ref[h] * fade[h : h + 1] + dot_tn(prev_ref[1, :, at_head[h]], weights)
        out_ref[:, at_head[h]] = total.T.astype(BF16)


def tuned(streams, lin_qkv, resid, w_out, w_qkv):
    rows, _, width = lin_qkv.shape
    nheads = width // HD
    group = nheads // 2
    full = w_out.shape[1]
    block = width // 2
    seq = lax.axis_index("seq")
    core = seq % 2
    shape = jax.ShapeDtypeStruct
    edges = [rows * sum(streams[:i]) // sum(streams) for i in range(len(streams) + 1)]
    cuts = list(zip(edges, edges[1:]))
    sizes = [b - a for a, b in cuts]
    last = len(cuts) - 1

    qkv = jnp.transpose(lin_qkv, (1, 0, 2))
    wqkv = jnp.transpose(w_qkv, (1, 0, 2))

    positions = seq * rows + jnp.arange(rows, dtype=jnp.int32)
    freq = 500000.0 ** (-(jnp.arange(HD // 2, dtype=F32) * 2.0 / HD))
    angle = positions.astype(F32)[:, None] * freq[None, :]
    cosine, sine = jnp.cos(angle), jnp.sin(angle)
    cos2 = jnp.concatenate([cosine, cosine], axis=1)
    sin2 = jnp.concatenate([-sine, sine], axis=1)

    with jax.named_scope("state"):
        states = shape((group, HD, HD), BF16)
        send, keep = call(
            state_body, (in_hbm(qkv),), (states, states), [IN_HBM],
            (
                pltpu.VMEM((2, rows, width // 2), BF16),
                pltpu.VMEM((2, rows, width // 2), BF16),
                pltpu.SemaphoreType.DMA((2, 2)),
            ),
            flops=2 * rows * width * HD, moved=4 * rows * width,
        )
        other = swapped(send, "seq", 1)
        chip_total = (keep.astype(F32) + other.astype(F32)).astype(BF16)
        by_x = swapped(chip_total, "seq", 2)
        by_y = swapped(chip_total, "seq", 4)
        by_xy = swapped(chip_total, "seq", 6)
    with jax.named_scope("intra"):
        columns = pltpu.VMEM((2, width, width), BF16)
        intra, q, w_other, w_mine = call(
            intra_body, (qkv, chip_total, cos2, sin2, in_hbm(w_out)),
            (shape((rows, width), F32), shape((rows, width), BF16), columns, columns),
            [ON_CHIP, ANYWHERE, ANYWHERE, ANYWHERE, IN_HBM], (pltpu.SemaphoreType.DMA((4,)),),
            flops=4 * rows * rows * width, moved=2 * width * full,
        )
        w_other, w_mine = in_vmem(w_other), in_vmem(w_mine)
    with jax.named_scope("prefix"):
        x_bit = ((seq // 2) % 2).astype(F32)
        y_bit = (seq // 4).astype(F32)
        chips = (
            by_x.astype(F32) * x_bit + by_y.astype(F32) * y_bit + by_xy.astype(F32) * y_bit
        )
        low = chips.astype(BF16)
        first_core = jnp.where(core == 0, keep, other)
        high = (chips + first_core.astype(F32)).astype(BF16)
        own_prefix = jnp.where(core == 0, low, high)
        other_prefix = swapped(jnp.where(core == 0, high, low), "seq", 1)

    scale = 1.0 / math.sqrt(HD * rows * lax.axis_size("seq"))
    halves = [shape((n, full // 2), BF16) for n in sizes]
    lin_scratch = pltpu.VMEM((rows, width), BF16)
    lin_inputs = (q, intra, own_prefix, other_prefix, w_other)
    with jax.named_scope("partials"):
        first_send = call(
            functools.partial(send_body, scale, cuts), lin_inputs, halves[0], scratch=(lin_scratch,),
            flops=sizes[0] * width * full, moved=width * full,
        )
        got = [lax.ppermute(first_send, "head", PAIR)]
        *made, w_here = call(
            functools.partial(mine_body, scale, cuts), (*lin_inputs, w_mine, resid, in_hbm(wqkv)),
            (*halves[1:], *halves, pltpu.VMEM(wqkv.shape, BF16)),
            [ON_CHIP] * 7 + [IN_HBM], (lin_scratch, pltpu.SemaphoreType.DMA((3 * full // width,))),
            flops=2 * rows * width * full, moved=6 * width * full,
        )
        sends, mines = made[:last], made[last:]
        w_here = in_vmem(w_here)

    def add(a, b):
        return call(add_body, (a, b), shape(a.shape, BF16), vmem=4, moved=3 * a.size)

    with jax.named_scope("mix"):
        totals, rests = [], []
        far = None
        for i in range(last + 1):
            if i > 0:
                ready = sends[i - 1]
                got.append(lax.ppermute(ready, "head", PAIR))
        for i in range(last + 1):
            partial = add(mines[i], got[i])
            if i > 0:
                pass
                totals.append(add(held, far))
            far = lax.ppermute(partial, "head", CROSS)
            held = partial
        totals.append(add(held, far))
        rests = [lax.ppermute(total, "head", PAIR) for total in totals]

    queries, kvs, prevs, accs = [], [], [], []
    cost = dict(flops=rows * full * 3 * width, moved=3 * width * full)
    with jax.named_scope("project"):
        for i in range(last):
            acc = shape((3, sizes[i], width), F32)
            accs.append(call(functools.partial(first_body, block), (totals[i], w_here), acc, **cost))
        acc, hidden = call(
            functools.partial(first_hidden_body, block, cuts), (totals[last], w_here, *totals[:last]),
            (shape((3, sizes[last], width), F32), shape((rows, width), BF16)), **cost,
        )
        accs.append(acc)
    for i in range(last + 1):
        n = sizes[i]
        with jax.named_scope("project"):
            kv, other = call(
                functools.partial(kv_body, block, cuts[i]),
                (totals[i], rests[i], w_here, accs[i], cos2, sin2, hidden),
                (shape((2, n, width), BF16), shape((n, width), BF16) if i < last else shape((n, HD), F32)),
                [ON_CHIP] * 6 + [ANYWHERE], **cost,
            )
            kvs.append(kv)
            queries.append(other)
            prevs.append(lax.ppermute(kv, "seq", [(i, (i + 1) % 8) for i in range(8)]))
    with jax.named_scope("attend"):
        inv = queries.pop()
        stat = shape((nheads, rows), F32)
        query, acc, top, total = call(
            functools.partial(early_body, block, cuts),
            (rests[last], w_here, acc, inv, cos2, sin2, *queries, *kvs, *prevs[:last]),
            (shape((sizes[last], width), BF16), shape((nheads, HD, rows), F32), stat, stat),
            flops=8 * rows * rows * width, moved=12 * rows * width,
        )
        attended = call(
            functools.partial(late_body, last + 1), (*queries, query, prevs[last], acc, top, total),
            shape((rows, width), BF16), flops=2 * rows * rows * width, moved=12 * rows * width,
        )
    return hidden, attended


def solution(mesh):
    line = mesh.shape["seq"] == 8 and mesh.shape["head"] == 4
    return jax.shard_map(
        functools.partial(tuned, STREAMS) if line else general,
        mesh=mesh,
        in_specs=(P("seq", None, "head"), P("seq", "head"), P("head", None), P(None, None, "head")),
        out_specs=(P("seq", "head"), P("seq", "head")),
        check_vma=False,
    )
```

```python
import functools
import math

import jax
import jax.numpy as jnp
from jax import lax
from jax.experimental import pallas as pl
from jax.experimental.pallas import tpu as pltpu
from jax.sharding import PartitionSpec as P

D = 4096
HD = 128
BF16 = jnp.bfloat16
F32 = jnp.float32
NEG = -1e30
FIRST, ACROSS, OWN, LAST, TURN = (1, 1), (2, 1, 1), (2, 1, 1), (2, 1, 1), (2, 1, 1)

PAIR = [(0, 1), (1, 0), (2, 3), (3, 2)]
CROSS = [(0, 3), (3, 0), (1, 2), (2, 1)]


def shifted(array, axis, by):
    devices = lax.axis_size(axis)
    pairs = [(i, i + by) for i in range(devices) if 0 <= i + by < devices]
    return lax.ppermute(array, axis, pairs)


def swapped(array, axis, bits):
    return lax.ppermute(array, axis, [(i, i ^ bits) for i in range(lax.axis_size(axis))])


def rotary(values, positions):
    half = values.shape[-1] // 2
    freq = 500000.0 ** (-(jnp.arange(half, dtype=jnp.float32) * 2.0 / values.shape[-1]))
    angle = positions.astype(jnp.float32)[:, None] * freq[None, :]
    cosine = jnp.cos(angle)[:, None, :]
    sine = jnp.sin(angle)[:, None, :]
    first = values[..., :half]
    second = values[..., half:]
    return jnp.concatenate(
        [first * cosine - second * sine, second * cosine + first * sine], axis=-1
    )


def general(lin_qkv, resid, w_out, w_qkv):
    tok_rows = lin_qkv.shape[0]
    local_width = lin_qkv.shape[2]
    nheads = local_width // HD
    n_seq = lax.axis_size("seq")
    own_index = lax.axis_index("seq")
    queries = lin_qkv[:, 0].reshape(tok_rows, nheads, HD)
    keys = lin_qkv[:, 1].reshape(tok_rows, nheads, HD)
    values = lin_qkv[:, 2].reshape(tok_rows, nheads, HD)
    own_state = jnp.einsum("thd,the->hde", keys, values, preferred_element_type=jnp.float32)
    piece = lax.all_gather(own_state[None], "seq", axis=0, tiled=True)
    keep = (jnp.arange(piece.shape[0], dtype=jnp.int32) < own_index).astype(jnp.float32)
    before = jnp.sum(piece * keep[:, None, None, None], axis=0)
    before = before.astype(jnp.bfloat16)
    causal = jnp.tril(jnp.ones((tok_rows, tok_rows), dtype=bool))
    scores = jnp.einsum("thd,shd->hts", queries, keys, preferred_element_type=jnp.float32)
    inner = jnp.where(causal[None], scores, 0.0).astype(jnp.bfloat16)
    total = jnp.einsum("hts,shd->thd", inner, values, preferred_element_type=jnp.float32)
    total = total + jnp.einsum("thd,hde->the", queries, before, preferred_element_type=jnp.float32)
    scale = 1.0 / math.sqrt(HD * tok_rows * n_seq)
    lin_out = (total * scale).astype(jnp.bfloat16).reshape(tok_rows, local_width)
    shared = lax.psum_scatter(
        lax.dot_general(
            w_out, lin_out, (((0,), (1,)), ((), ())), preferred_element_type=jnp.float32
        ).astype(jnp.bfloat16),
        "head",
        scatter_dimension=0,
        tiled=True,
    ).astype(jnp.float32)
    mixed_f = resid.astype(jnp.float32) + shared.T
    hidden = mixed_f.astype(jnp.bfloat16)
    flat_w = w_qkv.reshape(w_qkv.shape[0], 3 * local_width)
    squared = lax.psum(jnp.sum(mixed_f * mixed_f, axis=1), "head")
    normed = (mixed_f * lax.rsqrt(squared[:, None] / D + 1e-05)).astype(jnp.bfloat16)
    proj = jnp.dot(
        lax.all_gather(normed, "head", axis=1, tiled=True),
        flat_w,
        preferred_element_type=jnp.float32,
    )
    proj = proj.reshape(tok_rows, 3, nheads, HD)
    positions = own_index * tok_rows + jnp.arange(tok_rows, dtype=jnp.int32)
    query2 = rotary(proj[:, 0], positions).astype(jnp.bfloat16)
    key2 = rotary(proj[:, 1], positions).astype(jnp.bfloat16)
    value2 = proj[:, 2].astype(jnp.bfloat16)
    key_prev, value_prev = shifted((key2, value2), "seq", 1)
    score_scale = 1.0 / math.sqrt(HD)
    all_keys = jnp.concatenate([key_prev, key2], axis=0)
    all_values = jnp.concatenate([value_prev, value2], axis=0)
    logits = (
        jnp.einsum("thd,shd->hts", query2, all_keys, preferred_element_type=jnp.float32)
        * score_scale
    )
    allowed = jnp.concatenate([jnp.full((tok_rows, tok_rows), own_index > 0), causal], axis=1)
    logits = jnp.where(allowed[None], logits, -1e30)
    top = jnp.max(logits, axis=2, keepdims=True)
    expo = jnp.where(allowed[None], jnp.exp(logits - top), 0.0)
    weights = (expo / jnp.sum(expo, axis=2, keepdims=True)).astype(jnp.bfloat16)
    attended = jnp.einsum("hts,shd->thd", weights, all_values, preferred_element_type=jnp.float32)
    return (hidden, attended.astype(jnp.bfloat16).reshape(tok_rows, local_width))


def dot(a, b):
    return jnp.dot(a, b, preferred_element_type=F32)


def dot_nt(a, b):
    return lax.dot_general(a, b, (((1,), (1,)), ((), ())), preferred_element_type=F32)


def dot_tn(a, b):
    return lax.dot_general(a, b, (((0,), (0,)), ((), ())), preferred_element_type=F32)


def at(start, size):
    return pl.ds(pl.multiple_of(start, size), size)


ON_CHIP = pl.BlockSpec(memory_space=pltpu.VMEM)
IN_HBM = pl.BlockSpec(memory_space=pltpu.HBM)
ANYWHERE = pl.BlockSpec(memory_space=pl.ANY)


def call(body, ins, outs, in_specs=None, scratch=(), vmem=8, flops=0, moved=0, cost=0):
    return pl.pallas_call(
        body,
        in_specs=in_specs or [ON_CHIP] * len(ins),
        out_specs=jax.tree.map(lambda _: ON_CHIP, outs),
        out_shape=outs,
        scratch_shapes=scratch,
        compiler_params=pltpu.CompilerParams(vmem_limit_bytes=vmem * 2**20),
        cost_estimate=pl.CostEstimate(flops=cost, bytes_accessed=0, transcendentals=0),
    )(*ins)


def start_all(pairs, sems):
    copies = [pltpu.make_async_copy(a, b, sems.at[i]) for i, (a, b) in enumerate(pairs)]
    for copy in copies:
        copy.start()
    return copies


def in_hbm(array):
    return pltpu.with_memory_space_constraint(array, pltpu.HBM)


def in_vmem(array):
    return pltpu.with_memory_space_constraint(array, pltpu.VMEM)


def state_body(qkv_ref, send_ref, keep_ref, k_ref, v_ref, sems):
    core = lax.axis_index("seq") % 2
    count = send_ref.shape[0]
    wide = k_ref.shape[2]
    copies = []
    for slot in range(2):
        group = core if slot else 1 - core
        pair = []
        for plane, ref in ((1, k_ref), (2, v_ref)):
            copy = pltpu.make_async_copy(
                qkv_ref.at[plane, :, at(group * wide, wide)], ref.at[slot], sems.at[slot, plane - 1]
            )
            copy.start()
            pair.append(copy)
        copies.append(pair)
    for slot, out in ((0, send_ref), (1, keep_ref)):
        for copy in copies[slot]:
            copy.wait()
        for j in range(count):
            head = slice(j * HD, (j + 1) * HD)
            out[j] = dot_tn(k_ref[slot, :, head], v_ref[slot, :, head]).astype(BF16)


def intra_body(qkv_ref, after, cos_ref, sin_ref, w_ref, o_ref, q_ref, w_other_ref, w_mine_ref, sems):
    _, mine, other = quarters()
    width = w_mine_ref.shape[2]
    copies = start_all(
        [
            (w_ref.at[:, at(which[p] * width, width)], to.at[p])
            for which, to in ((other, w_other_ref), (mine, w_mine_ref))
            for p in range(2)
        ],
        sems,
    )
    rows = qkv_ref.shape[1]
    ahead = lax.broadcasted_iota(jnp.int32, (rows, rows), 1) > lax.broadcasted_iota(
        jnp.int32, (rows, rows), 0
    )
    q_ref[...] = qkv_ref[0]
    for h in range(qkv_ref.shape[2] // HD):
        head = slice(h * HD, (h + 1) * HD)
        scores = dot_nt(qkv_ref[0, :, head], qkv_ref[1, :, head])
        inner = jnp.where(ahead, 0.0, scores).astype(BF16)
        o_ref[:, head] = dot(inner, qkv_ref[2, :, head])
    for copy in copies:
        copy.wait()


def quarters():
    z = lax.axis_index("head")
    edge = (z == 0) | (z == 3)
    outer, inner = (0, 3), (1, 2)
    mine = [jnp.where(edge, a, b) for a, b in zip(outer, inner)]
    other = [jnp.where(edge, b, a) for a, b in zip(outer, inner)]
    return z, mine, other


def lin_out_rows(scale, rows, q_ref, intra_ref, own_ref, other_ref, lin_ref):
    core = lax.axis_index("seq") % 2
    count = own_ref.shape[0]
    for ref, group in ((own_ref, core), (other_ref, 1 - core)):
        for j in range(count):
            head = at((group * count + j) * HD, HD)
            total = intra_ref[rows, head] + dot(q_ref[rows, head], ref[j])
            lin_ref[rows, head] = (total * scale).astype(BF16)


def send_body(scale, cuts, q_ref, intra_ref, own_ref, other_ref, w_ref, send_ref, lin_ref):
    rows = slice(*cuts[0])
    lin_out_rows(scale, rows, q_ref, intra_ref, own_ref, other_ref, lin_ref)
    width = w_ref.shape[2]
    block = width // 2
    for p in range(2):
        for n in range(2):
            to = slice(p * width + n * block, p * width + (n + 1) * block)
            send_ref[:, to] = dot(lin_ref[rows], w_ref[p, :, n * block : (n + 1) * block]).astype(BF16)


def mine_body(scale, cuts, *refs):
    q_ref, intra_ref, own_ref, other_ref, w_other_ref, w_mine_ref, r_ref, w_qkv_ref, after = refs[:9]
    count = len(cuts)
    send_refs, mine_refs = refs[9 : 8 + count], refs[8 + count : 8 + 2 * count]
    w_qkv_to_ref, lin_ref, sems = refs[8 + 2 * count :]
    z, mine, _ = quarters()
    width = w_mine_ref.shape[2]
    block = width // 2
    copies = start_all(
        [
            (w_qkv_ref.at[j, pl.ds(i, width)], w_qkv_to_ref.at[j, pl.ds(i, width)])
            for j in range(3)
            for i in range(0, w_qkv_ref.shape[1], width)
        ],
        sems,
    )
    lin_out_rows(scale, slice(None), q_ref, intra_ref, own_ref, other_ref, lin_ref)
    skip = cuts[0][1]
    for p in range(2):
        for n in range(2):
            part = slice(n * block, (n + 1) * block)
            to = slice(p * width + n * block, p * width + (n + 1) * block)
            product = dot(lin_ref[skip:], w_other_ref[p, :, part]).astype(BF16)
            for (a, b), ref in zip(cuts[1:], send_refs):
                ref[:, to] = product[a - skip : b - skip]
    for p in range(2):
        for n in range(2):
            part = slice(n * block, (n + 1) * block)
            to = slice(p * width + n * block, p * width + (n + 1) * block)
            product = dot(lin_ref[...], w_mine_ref[p, :, part])
            own = jnp.where(mine[p] == z, r_ref[:, part].astype(F32), 0.0)
            product = (product + own).astype(BF16)
            for (a, b), ref in zip(cuts, mine_refs):
                ref[:, to] = product[a:b]
    for copy in copies:
        copy.wait()


def overlaps(groups, rows):
    found = []
    for i, (a, b) in enumerate(groups):
        low, high = max(a, rows[0]), min(b, rows[1])
        if low < high:
            found.append((i, slice(low - a, high - a), slice(low - rows[0], high - rows[0])))
    return found


def add_body(places, *refs):
    *refs, o_ref = refs
    for i, (_, source, target) in enumerate(places):
        total = refs[2 * i][source].astype(F32) + refs[2 * i + 1][source].astype(F32)
        o_ref[target] = total.astype(BF16)


def two_quarters(x, w_ref, plane, which, to):
    width = x.shape[1] // 2
    low = dot(x[:, :width], w_ref[plane, at(which[0] * width, width), to])
    return low + dot(x[:, width:], w_ref[plane, at(which[1] * width, width), to])


def joined(refs):
    return refs[0] if len(refs) == 1 else jnp.concatenate([ref[...] for ref in refs], axis=0)


def first_body(block, w_ref, *refs):
    *x_refs, acc_ref = refs
    _, mine, _ = quarters()
    x = joined(x_refs)
    for plane in range(3):
        for n in range(acc_ref.shape[2] // block):
            to = slice(n * block, (n + 1) * block)
            acc_ref[plane, :, to] = two_quarters(x, w_ref, plane, mine, to)


def first_hidden_body(block, cuts, count, w_ref, *refs):
    *total_refs, acc_ref, hidden_ref = refs
    width = acc_ref.shape[2]
    own = at((lax.axis_index("head") // 2) * width, width)
    for (a, b), ref in zip(cuts, total_refs):
        hidden_ref[a:b] = ref[:, own]
    first_body(block, w_ref, *total_refs[-count:], acc_ref)


def finish(block, plane, x, w_ref, acc_ref, rows, inv, cos, sin, out_ref):
    _, _, other = quarters()
    for n in range(acc_ref.shape[2] // block):
        to = slice(n * block, (n + 1) * block)
        total = (acc_ref[plane, rows, to] + two_quarters(x, w_ref, plane, other, to)) * inv
        if plane == 2:
            out_ref[:, to] = total.astype(BF16)
            continue
        for h in range(block // HD):
            value = total[:, h * HD : (h + 1) * HD]
            turned = value * cos + pltpu.roll(value, HD // 2, 1) * sin
            out_ref[:, n * block + h * HD : n * block + (h + 1) * HD] = turned.astype(BF16)


def kv_body(block, rows, own, count, *refs):
    t_refs, x_refs = refs[:count], refs[count : 2 * count]
    w_ref, acc_ref, cos_ref, sin_ref, _, kv_ref, rest_ref = refs[2 * count :]
    x_ref = joined(x_refs)
    t = joined(t_refs)[...].astype(F32)
    x = x_ref[...].astype(F32)
    total = jnp.sum(t * t + x * x, axis=1, keepdims=True)
    inv = lax.rsqrt(total / D + 1e-05)
    cos, sin = cos_ref[slice(*rows)], sin_ref[slice(*rows)]
    for plane in (1, 2):
        finish(block, plane, x_ref, w_ref, acc_ref, own, inv, cos, sin, kv_ref.at[plane - 1])
    if rest_ref.dtype == BF16:
        finish(block, 0, x_ref, w_ref, acc_ref, own, inv, cos, sin, rest_ref)
    else:
        rest_ref[...] = jnp.broadcast_to(inv, rest_ref.shape)


SCORE = 1.0 / math.sqrt(HD)


def stacked(refs, *where):
    return jnp.concatenate([ref[where] for ref in refs], axis=0)


def early_body(block, rows, before, q_count, x_count, inv_count, kv_count, *refs):
    w_ref, acc_in_ref, cos_ref, sin_ref = refs[:4]
    refs = refs[4:]
    x_refs, refs = refs[:x_count], refs[x_count:]
    inv_refs, refs = refs[:inv_count], refs[inv_count:]
    q_refs, refs = refs[:q_count], refs[q_count:]
    kv_refs, prev_refs = refs[:kv_count], refs[kv_count : 2 * kv_count - 1]
    q_ref, acc_ref, top_ref, sum_ref = refs[2 * kv_count - 1 :]
    inv = joined(inv_refs)[:, :1]
    cos, sin = cos_ref[slice(*rows)], sin_ref[slice(*rows)]
    finish(block, 0, joined(x_refs), w_ref, acc_in_ref, slice(None), inv, cos, sin, q_ref)
    q_refs = (*q_refs, q_ref)
    has_prev = lax.axis_index("seq") > 0
    shape = (before + rows[1], rows[1])
    key = lax.broadcasted_iota(jnp.int32, shape, 0)
    query = lax.broadcasted_iota(jnp.int32, shape, 1)
    allowed = ((key < before) & has_prev) | ((key >= before) & (key - before <= query))
    for h in range(q_ref.shape[1] // HD):
        head = slice(h * HD, (h + 1) * HD)
        keys = stacked((*prev_refs, *kv_refs), 0, slice(None), head)
        values = stacked((*prev_refs, *kv_refs), 1, slice(None), head)
        logits = dot_nt(keys, stacked(q_refs, slice(None), head)) * SCORE
        logits = jnp.where(allowed, logits, NEG)
        top = jnp.max(logits, axis=0, keepdims=True)
        expo = jnp.where(allowed, jnp.exp(logits - top), 0.0)
        top_ref[h : h + 1] = top
        sum_ref[h : h + 1] = jnp.sum(expo, axis=0, keepdims=True)
        acc_ref[h] = dot_tn(values, expo.astype(BF16))


def late_body(count, *refs):
    q_refs, (prev_ref, acc_ref, top_ref, sum_ref, out_ref) = refs[:count], refs[count:]
    has_prev = lax.axis_index("seq") > 0
    heads = range(out_ref.shape[1] // HD)
    at_head = [slice(h * HD, (h + 1) * HD) for h in heads]
    logits = [
        jnp.where(has_prev, dot_nt(prev_ref[0, :, at], stacked(q_refs, slice(None), at)) * SCORE, NEG)
        for at in at_head
    ]
    highest = jnp.concatenate([jnp.max(x, axis=0, keepdims=True) for x in logits], axis=0)
    top = jnp.maximum(top_ref[...], highest)
    fade = jnp.exp(top_ref[...] - top)
    expo = [jnp.where(has_prev, jnp.exp(logits[h] - top[h : h + 1]), 0.0) for h in heads]
    sums = jnp.concatenate([jnp.sum(x, axis=0, keepdims=True) for x in expo], axis=0)
    inverse = 1.0 / (sum_ref[...] * fade + sums)
    fade = fade * inverse
    for h in heads:
        weights = (expo[h] * inverse[h : h + 1]).astype(BF16)
        total = acc_ref[h] * fade[h : h + 1] + dot_tn(prev_ref[1, :, at_head[h]], weights)
        out_ref[:, at_head[h]] = total.T.astype(BF16)


def tuned(lin_qkv, resid, w_out, w_qkv):
    rows, _, width = lin_qkv.shape
    nheads = width // HD
    group = nheads // 2
    full = w_out.shape[1]
    block = width // 2
    seq = lax.axis_index("seq")
    core = seq % 2
    shape = jax.ShapeDtypeStruct

    def shared(shares):
        edges = [rows * sum(shares[:i]) // sum(shares) for i in range(len(shares) + 1)]
        return list(zip(edges, edges[1:]))

    cuts, across, owns, ends, turns = (shared(x) for x in (FIRST, ACROSS, OWN, LAST, TURN))
    sizes = [b - a for a, b in cuts]
    last = len(cuts) - 1

    qkv = jnp.transpose(lin_qkv, (1, 0, 2))
    wqkv = jnp.transpose(w_qkv, (1, 0, 2))

    positions = seq * rows + jnp.arange(rows, dtype=jnp.int32)
    freq = 500000.0 ** (-(jnp.arange(HD // 2, dtype=F32) * 2.0 / HD))
    angle = positions.astype(F32)[:, None] * freq[None, :]
    cosine, sine = jnp.cos(angle), jnp.sin(angle)
    cos2 = jnp.concatenate([cosine, cosine], axis=1)
    sin2 = jnp.concatenate([-sine, sine], axis=1)

    with jax.named_scope("state"):
        states = shape((group, HD, HD), BF16)
        send, keep = call(
            state_body, (in_hbm(qkv),), (states, states), [IN_HBM],
            (
                pltpu.VMEM((2, rows, width // 2), BF16),
                pltpu.VMEM((2, rows, width // 2), BF16),
                pltpu.SemaphoreType.DMA((2, 2)),
            ),
            flops=2 * rows * width * HD, moved=4 * rows * width,
        )
        other = swapped(send, "seq", 1)
        chip_total = (keep.astype(F32) + other.astype(F32)).astype(BF16)
        by_x = swapped(chip_total, "seq", 2)
        by_y = swapped(chip_total, "seq", 4)
        by_xy = swapped(chip_total, "seq", 6)
    with jax.named_scope("intra"):
        columns = pltpu.VMEM((2, width, width), BF16)
        intra, q, w_other, w_mine = call(
            intra_body, (qkv, chip_total, cos2, sin2, in_hbm(w_out)),
            (shape((rows, width), F32), shape((rows, width), BF16), columns, columns),
            [ON_CHIP, ANYWHERE, ANYWHERE, ANYWHERE, IN_HBM], (pltpu.SemaphoreType.DMA((4,)),),
            flops=4 * rows * rows * width, moved=2 * width * full,
        )
        w_other, w_mine = in_vmem(w_other), in_vmem(w_mine)
    with jax.named_scope("prefix"):
        x_bit = ((seq // 2) % 2).astype(F32)
        y_bit = (seq // 4).astype(F32)
        chips = (
            by_x.astype(F32) * x_bit + by_y.astype(F32) * y_bit + by_xy.astype(F32) * y_bit
        )
        low = chips.astype(BF16)
        first_core = jnp.where(core == 0, keep, other)
        high = (chips + first_core.astype(F32)).astype(BF16)
        own_prefix = jnp.where(core == 0, low, high)
        other_prefix = swapped(jnp.where(core == 0, high, low), "seq", 1)

    scale = 1.0 / math.sqrt(HD * rows * lax.axis_size("seq"))
    halves = [shape((n, full // 2), BF16) for n in sizes]
    lin_scratch = pltpu.VMEM((rows, width), BF16)
    lin_inputs = (q, intra, own_prefix, other_prefix, w_other)
    with jax.named_scope("partials"):
        first_send = call(
            functools.partial(send_body, scale, cuts), lin_inputs, halves[0], scratch=(lin_scratch,),
            flops=sizes[0] * width * full, moved=width * full,
        )
        got = [lax.ppermute(first_send, "head", PAIR)]
        *made, w_here = call(
            functools.partial(mine_body, scale, cuts), (*lin_inputs, w_mine, resid, in_hbm(wqkv), first_send),
            (*halves[1:], *halves, pltpu.VMEM(wqkv.shape, BF16)),
            [ON_CHIP] * 7 + [IN_HBM, ANYWHERE], (lin_scratch, pltpu.SemaphoreType.DMA((3 * full // width,))),
            flops=2 * rows * width * full, moved=6 * width * full,
        )
        sends, mines = made[:last], made[last:]
        w_here = in_vmem(w_here)

    def added(lefts, rights, groups, target, after=()):
        places = overlaps(groups, target)
        ins = [x for i, _, _ in places for x in (lefts[i], rights[i])]
        out = shape((target[1] - target[0], full // 2), BF16)
        specs = [ON_CHIP] * len(ins) + [ANYWHERE] * len(after)
        return call(functools.partial(add_body, places), (*ins, *after), out, specs, vmem=4, moved=3 * out.size)

    with jax.named_scope("mix"):
        got += [lax.ppermute(send, "head", PAIR) for send in sends]
        sums, far = [], []
        for i, group in enumerate(across):
            part = added(mines, got, cuts, group, sums[-1:])
            for j in {2: (1,)}.get(i, ()):
                part, far[j] = lax.optimization_barrier((part, far[j]))
            sums.append(part)
            far.append(lax.ppermute(part, "head", CROSS))

    def inside(group):
        return [i for i, (a, b) in enumerate(ends) if group[0] <= a and b <= group[1]]

    totals, rests, accs = [], [], []
    queries, invs, kvs, prevs = [], [], [], []
    ring = [(i, (i + 1) % lax.axis_size("seq")) for i in range(lax.axis_size("seq"))]

    def turn(group):
        members = inside(group)
        (k, own, _), = overlaps(owns, group)
        n = group[1] - group[0]
        tail = k == len(owns) - 1
        kv, other = call(
            functools.partial(kv_body, block, group, own, len(members)),
            (*(totals[i] for i in members), *(rests[i] for i in members), w_here, accs[k], cos2, sin2, accs[-1]),
            (shape((2, n, width), BF16), shape((n, HD), F32) if tail else shape((n, width), BF16)),
            [ON_CHIP] * (2 * len(members) + 4) + [ANYWHERE],
        )
        kvs.append(kv)
        (invs if tail else queries).append(other)
        prevs.append(lax.ppermute(kv, "seq", ring))

    for k, group in enumerate(owns):
        members = inside(group)
        before = totals[-1:]
        if k == len(owns) - 1:
            with jax.named_scope("project"):
                for early in turns:
                    if early[1] <= owns[0][1]:
                        turn(early)
            before = kvs[-1:] and before
        with jax.named_scope("mix"):
            for i in members:
                totals.append(added(sums, far, across, ends[i], before))
            rests += [lax.ppermute(totals[i], "head", PAIR) for i in members]
        with jax.named_scope("project"):
            acc = shape((3, group[1] - group[0], width), F32)
            if k < len(owns) - 1:
                inputs = [totals[i] for i in members]
                accs.append(call(functools.partial(first_body, block), (w_here, *inputs), acc))
                continue
            acc, hidden = call(
                functools.partial(first_hidden_body, block, ends, len(members)), (w_here, *totals),
                (acc, shape((rows, width), BF16)),
            )
            accs.append(acc)
    with jax.named_scope("project"):
        for group in turns[len(kvs) :]:
            turn(group)
    with jax.named_scope("attend"):
        stat = shape((nheads, rows), F32)
        tail = owns[-1]
        members = [rests[i] for i in inside(tail)]
        query, acc, top, total = call(
            functools.partial(early_body, block, tail, turns[-1][0], len(queries), len(members), len(invs), len(kvs)),
            (w_here, accs[-1], cos2, sin2, *members, *invs, *queries, *kvs, *prevs[:-1]),
            (shape((tail[1] - tail[0], width), BF16), shape((nheads, HD, rows), F32), stat, stat),
            flops=8 * rows * rows * width, moved=12 * rows * width,
        )
        queries.append(query)
        attended = call(
            functools.partial(late_body, len(queries)), (*queries, prevs[-1], acc, top, total),
            shape((rows, width), BF16), flops=2 * rows * rows * width, moved=12 * rows * width,
        )
    return hidden, attended


def solution(mesh):
    line = mesh.shape["seq"] == 8 and mesh.shape["head"] == 4
    return jax.shard_map(
        tuned if line else general,
        mesh=mesh,
        in_specs=(P("seq", None, "head"), P("seq", "head"), P("head", None), P(None, None, "head")),
        out_specs=(P("seq", "head"), P("seq", "head")),
        check_vma=False,
    )
```

```python
import functools
import math

import jax
import jax.numpy as jnp
from jax import lax
from jax.experimental import pallas as pl
from jax.experimental.pallas import tpu as pltpu
from jax.sharding import PartitionSpec as P

D = 4096
HD = 128
BF16 = jnp.bfloat16
F32 = jnp.float32
NEG = -1e30
FIRST, ACROSS, OWN, LAST, TURN = (1, 1), (2, 1, 1), (2, 1, 1), (2, 1, 1), (2, 1, 1)

PAIR = [(0, 1), (1, 0), (2, 3), (3, 2)]
CROSS = [(0, 3), (3, 0), (1, 2), (2, 1)]


def shifted(array, axis, by):
    devices = lax.axis_size(axis)
    pairs = [(i, i + by) for i in range(devices) if 0 <= i + by < devices]
    return lax.ppermute(array, axis, pairs)


def swapped(array, axis, bits):
    return lax.ppermute(array, axis, [(i, i ^ bits) for i in range(lax.axis_size(axis))])


def rotary(values, positions):
    half = values.shape[-1] // 2
    freq = 500000.0 ** (-(jnp.arange(half, dtype=jnp.float32) * 2.0 / values.shape[-1]))
    angle = positions.astype(jnp.float32)[:, None] * freq[None, :]
    cosine = jnp.cos(angle)[:, None, :]
    sine = jnp.sin(angle)[:, None, :]
    first = values[..., :half]
    second = values[..., half:]
    return jnp.concatenate(
        [first * cosine - second * sine, second * cosine + first * sine], axis=-1
    )


def general(lin_qkv, resid, w_out, w_qkv):
    tok_rows = lin_qkv.shape[0]
    local_width = lin_qkv.shape[2]
    nheads = local_width // HD
    n_seq = lax.axis_size("seq")
    own_index = lax.axis_index("seq")
    queries = lin_qkv[:, 0].reshape(tok_rows, nheads, HD)
    keys = lin_qkv[:, 1].reshape(tok_rows, nheads, HD)
    values = lin_qkv[:, 2].reshape(tok_rows, nheads, HD)
    own_state = jnp.einsum("thd,the->hde", keys, values, preferred_element_type=jnp.float32)
    piece = lax.all_gather(own_state[None], "seq", axis=0, tiled=True)
    keep = (jnp.arange(piece.shape[0], dtype=jnp.int32) < own_index).astype(jnp.float32)
    before = jnp.sum(piece * keep[:, None, None, None], axis=0)
    before = before.astype(jnp.bfloat16)
    causal = jnp.tril(jnp.ones((tok_rows, tok_rows), dtype=bool))
    scores = jnp.einsum("thd,shd->hts", queries, keys, preferred_element_type=jnp.float32)
    inner = jnp.where(causal[None], scores, 0.0).astype(jnp.bfloat16)
    total = jnp.einsum("hts,shd->thd", inner, values, preferred_element_type=jnp.float32)
    total = total + jnp.einsum("thd,hde->the", queries, before, preferred_element_type=jnp.float32)
    scale = 1.0 / math.sqrt(HD * tok_rows * n_seq)
    lin_out = (total * scale).astype(jnp.bfloat16).reshape(tok_rows, local_width)
    shared = lax.psum_scatter(
        lax.dot_general(
            w_out, lin_out, (((0,), (1,)), ((), ())), preferred_element_type=jnp.float32
        ).astype(jnp.bfloat16),
        "head",
        scatter_dimension=0,
        tiled=True,
    ).astype(jnp.float32)
    mixed_f = resid.astype(jnp.float32) + shared.T
    hidden = mixed_f.astype(jnp.bfloat16)
    flat_w = w_qkv.reshape(w_qkv.shape[0], 3 * local_width)
    squared = lax.psum(jnp.sum(mixed_f * mixed_f, axis=1), "head")
    normed = (mixed_f * lax.rsqrt(squared[:, None] / D + 1e-05)).astype(jnp.bfloat16)
    proj = jnp.dot(
        lax.all_gather(normed, "head", axis=1, tiled=True),
        flat_w,
        preferred_element_type=jnp.float32,
    )
    proj = proj.reshape(tok_rows, 3, nheads, HD)
    positions = own_index * tok_rows + jnp.arange(tok_rows, dtype=jnp.int32)
    query2 = rotary(proj[:, 0], positions).astype(jnp.bfloat16)
    key2 = rotary(proj[:, 1], positions).astype(jnp.bfloat16)
    value2 = proj[:, 2].astype(jnp.bfloat16)
    key_prev, value_prev = shifted((key2, value2), "seq", 1)
    score_scale = 1.0 / math.sqrt(HD)
    all_keys = jnp.concatenate([key_prev, key2], axis=0)
    all_values = jnp.concatenate([value_prev, value2], axis=0)
    logits = (
        jnp.einsum("thd,shd->hts", query2, all_keys, preferred_element_type=jnp.float32)
        * score_scale
    )
    allowed = jnp.concatenate([jnp.full((tok_rows, tok_rows), own_index > 0), causal], axis=1)
    logits = jnp.where(allowed[None], logits, -1e30)
    top = jnp.max(logits, axis=2, keepdims=True)
    expo = jnp.where(allowed[None], jnp.exp(logits - top), 0.0)
    weights = (expo / jnp.sum(expo, axis=2, keepdims=True)).astype(jnp.bfloat16)
    attended = jnp.einsum("hts,shd->thd", weights, all_values, preferred_element_type=jnp.float32)
    return (hidden, attended.astype(jnp.bfloat16).reshape(tok_rows, local_width))


def dot(a, b):
    return jnp.dot(a, b, preferred_element_type=F32)


def dot_nt(a, b):
    return lax.dot_general(a, b, (((1,), (1,)), ((), ())), preferred_element_type=F32)


def dot_tn(a, b):
    return lax.dot_general(a, b, (((0,), (0,)), ((), ())), preferred_element_type=F32)


def at(start, size):
    return pl.ds(pl.multiple_of(start, size), size)


ON_CHIP = pl.BlockSpec(memory_space=pltpu.VMEM)
IN_HBM = pl.BlockSpec(memory_space=pltpu.HBM)
ANYWHERE = pl.BlockSpec(memory_space=pl.ANY)


def call(body, ins, outs, in_specs=None, scratch=(), vmem=8, flops=0, moved=0, cost=0):
    return pl.pallas_call(
        body,
        in_specs=in_specs or [ON_CHIP] * len(ins),
        out_specs=jax.tree.map(lambda _: ON_CHIP, outs),
        out_shape=outs,
        scratch_shapes=scratch,
        compiler_params=pltpu.CompilerParams(vmem_limit_bytes=vmem * 2**20),
        cost_estimate=pl.CostEstimate(flops=cost, bytes_accessed=0, transcendentals=0),
    )(*ins)


def start_all(pairs, sems):
    copies = [pltpu.make_async_copy(a, b, sems.at[i]) for i, (a, b) in enumerate(pairs)]
    for copy in copies:
        copy.start()
    return copies


def in_hbm(array):
    return pltpu.with_memory_space_constraint(array, pltpu.HBM)


def in_vmem(array):
    return pltpu.with_memory_space_constraint(array, pltpu.VMEM)


def state_body(other, qkv_ref, after, state_ref, k_ref, v_ref, sems):
    core = lax.axis_index("seq") % 2
    group = 1 - core if other else core
    wide = k_ref.shape[1]
    copies = start_all(
        [
            (qkv_ref.at[plane, :, at(group * wide, wide)], ref)
            for plane, ref in ((1, k_ref), (2, v_ref))
        ],
        sems,
    )
    for copy in copies:
        copy.wait()
    for j in range(state_ref.shape[0]):
        head = slice(j * HD, (j + 1) * HD)
        state_ref[j] = dot_tn(k_ref[:, head], v_ref[:, head]).astype(BF16)


def intra_body(qkv_ref, after, cos_ref, sin_ref, w_ref, o_ref, q_ref, w_other_ref, w_mine_ref, sems):
    _, mine, other = quarters()
    width = w_mine_ref.shape[2]
    copies = start_all(
        [
            (w_ref.at[:, at(which[p] * width, width)], to.at[p])
            for which, to in ((other, w_other_ref), (mine, w_mine_ref))
            for p in range(2)
        ],
        sems,
    )
    rows = qkv_ref.shape[1]
    ahead = lax.broadcasted_iota(jnp.int32, (rows, rows), 1) > lax.broadcasted_iota(
        jnp.int32, (rows, rows), 0
    )
    q_ref[...] = qkv_ref[0]
    for h in range(qkv_ref.shape[2] // HD):
        head = slice(h * HD, (h + 1) * HD)
        scores = dot_nt(qkv_ref[0, :, head], qkv_ref[1, :, head])
        inner = jnp.where(ahead, 0.0, scores).astype(BF16)
        o_ref[:, head] = dot(inner, qkv_ref[2, :, head])
    for copy in copies:
        copy.wait()


def quarters():
    z = lax.axis_index("head")
    edge = (z == 0) | (z == 3)
    outer, inner = (0, 3), (1, 2)
    mine = [jnp.where(edge, a, b) for a, b in zip(outer, inner)]
    other = [jnp.where(edge, b, a) for a, b in zip(outer, inner)]
    return z, mine, other


def lin_out_rows(scale, rows, q_ref, intra_ref, own_ref, other_ref, lin_ref):
    core = lax.axis_index("seq") % 2
    count = own_ref.shape[0]
    for ref, group in ((own_ref, core), (other_ref, 1 - core)):
        for j in range(count):
            head = at((group * count + j) * HD, HD)
            total = intra_ref[rows, head] + dot(q_ref[rows, head], ref[j])
            lin_ref[rows, head] = (total * scale).astype(BF16)


def send_body(scale, cuts, q_ref, intra_ref, own_ref, other_ref, w_ref, send_ref, lin_ref):
    rows = slice(*cuts[0])
    lin_out_rows(scale, rows, q_ref, intra_ref, own_ref, other_ref, lin_ref)
    width = w_ref.shape[2]
    block = width // 2
    for p in range(2):
        for n in range(2):
            to = slice(p * width + n * block, p * width + (n + 1) * block)
            send_ref[:, to] = dot(lin_ref[rows], w_ref[p, :, n * block : (n + 1) * block]).astype(BF16)


def mine_body(scale, cuts, *refs):
    q_ref, intra_ref, own_ref, other_ref, w_other_ref, w_mine_ref, r_ref, w_qkv_ref, after = refs[:9]
    count = len(cuts)
    send_refs, mine_refs = refs[9 : 8 + count], refs[8 + count : 8 + 2 * count]
    w_qkv_to_ref, lin_ref, sems = refs[8 + 2 * count :]
    z, mine, _ = quarters()
    width = w_mine_ref.shape[2]
    block = width // 2
    copies = start_all(
        [
            (w_qkv_ref.at[j, pl.ds(i, width)], w_qkv_to_ref.at[j, pl.ds(i, width)])
            for j in range(3)
            for i in range(0, w_qkv_ref.shape[1], width)
        ],
        sems,
    )
    lin_out_rows(scale, slice(None), q_ref, intra_ref, own_ref, other_ref, lin_ref)
    skip = cuts[0][1]
    for p in range(2):
        for n in range(2):
            part = slice(n * block, (n + 1) * block)
            to = slice(p * width + n * block, p * width + (n + 1) * block)
            product = dot(lin_ref[skip:], w_other_ref[p, :, part]).astype(BF16)
            for (a, b), ref in zip(cuts[1:], send_refs):
                ref[:, to] = product[a - skip : b - skip]
    for p in range(2):
        for n in range(2):
            part = slice(n * block, (n + 1) * block)
            to = slice(p * width + n * block, p * width + (n + 1) * block)
            product = dot(lin_ref[...], w_mine_ref[p, :, part])
            own = jnp.where(mine[p] == z, r_ref[:, part].astype(F32), 0.0)
            product = (product + own).astype(BF16)
            for (a, b), ref in zip(cuts, mine_refs):
                ref[:, to] = product[a:b]
    for copy in copies:
        copy.wait()


def overlaps(groups, rows):
    found = []
    for i, (a, b) in enumerate(groups):
        low, high = max(a, rows[0]), min(b, rows[1])
        if low < high:
            found.append((i, slice(low - a, high - a), slice(low - rows[0], high - rows[0])))
    return found


def add_body(places, *refs):
    *refs, o_ref = refs
    for i, (_, source, target) in enumerate(places):
        total = refs[2 * i][source].astype(F32) + refs[2 * i + 1][source].astype(F32)
        o_ref[target] = total.astype(BF16)


def two_quarters(x, w_ref, plane, which, to):
    width = x.shape[1] // 2
    low = dot(x[:, :width], w_ref[plane, at(which[0] * width, width), to])
    return low + dot(x[:, width:], w_ref[plane, at(which[1] * width, width), to])


def joined(refs):
    return refs[0] if len(refs) == 1 else jnp.concatenate([ref[...] for ref in refs], axis=0)


def first_body(block, w_ref, *refs):
    *x_refs, acc_ref = refs
    _, mine, _ = quarters()
    x = joined(x_refs)
    for plane in range(3):
        for n in range(acc_ref.shape[2] // block):
            to = slice(n * block, (n + 1) * block)
            acc_ref[plane, :, to] = two_quarters(x, w_ref, plane, mine, to)


def first_hidden_body(block, cuts, count, w_ref, *refs):
    *total_refs, acc_ref, hidden_ref = refs
    width = acc_ref.shape[2]
    own = at((lax.axis_index("head") // 2) * width, width)
    for (a, b), ref in zip(cuts, total_refs):
        hidden_ref[a:b] = ref[:, own]
    first_body(block, w_ref, *total_refs[-count:], acc_ref)


def finish(block, plane, x, w_ref, acc_ref, rows, inv, cos, sin, out_ref):
    _, _, other = quarters()
    for n in range(acc_ref.shape[2] // block):
        to = slice(n * block, (n + 1) * block)
        total = (acc_ref[plane, rows, to] + two_quarters(x, w_ref, plane, other, to)) * inv
        if plane == 2:
            out_ref[:, to] = total.astype(BF16)
            continue
        for h in range(block // HD):
            value = total[:, h * HD : (h + 1) * HD]
            turned = value * cos + pltpu.roll(value, HD // 2, 1) * sin
            out_ref[:, n * block + h * HD : n * block + (h + 1) * HD] = turned.astype(BF16)


def kv_body(block, rows, own, count, *refs):
    t_refs, x_refs = refs[:count], refs[count : 2 * count]
    w_ref, acc_ref, cos_ref, sin_ref, _, kv_ref, rest_ref = refs[2 * count :]
    x_ref = joined(x_refs)
    t = joined(t_refs)[...].astype(F32)
    x = x_ref[...].astype(F32)
    total = jnp.sum(t * t + x * x, axis=1, keepdims=True)
    inv = lax.rsqrt(total / D + 1e-05)
    cos, sin = cos_ref[slice(*rows)], sin_ref[slice(*rows)]
    for plane in (1, 2):
        finish(block, plane, x_ref, w_ref, acc_ref, own, inv, cos, sin, kv_ref.at[plane - 1])
    if rest_ref.dtype == BF16:
        finish(block, 0, x_ref, w_ref, acc_ref, own, inv, cos, sin, rest_ref)
    else:
        rest_ref[...] = jnp.broadcast_to(inv, rest_ref.shape)


SCORE = 1.0 / math.sqrt(HD)


def stacked(refs, *where):
    return jnp.concatenate([ref[where] for ref in refs], axis=0)


def early_body(block, rows, before, q_count, x_count, inv_count, kv_count, *refs):
    w_ref, acc_in_ref, cos_ref, sin_ref = refs[:4]
    refs = refs[4:]
    x_refs, refs = refs[:x_count], refs[x_count:]
    inv_refs, refs = refs[:inv_count], refs[inv_count:]
    q_refs, refs = refs[:q_count], refs[q_count:]
    kv_refs, prev_refs = refs[:kv_count], refs[kv_count : 2 * kv_count - 1]
    q_ref, acc_ref, top_ref, sum_ref = refs[2 * kv_count - 1 :]
    inv = joined(inv_refs)[:, :1]
    cos, sin = cos_ref[slice(*rows)], sin_ref[slice(*rows)]
    finish(block, 0, joined(x_refs), w_ref, acc_in_ref, slice(None), inv, cos, sin, q_ref)
    q_refs = (*q_refs, q_ref)
    has_prev = lax.axis_index("seq") > 0
    shape = (before + rows[1], rows[1])
    key = lax.broadcasted_iota(jnp.int32, shape, 0)
    query = lax.broadcasted_iota(jnp.int32, shape, 1)
    allowed = ((key < before) & has_prev) | ((key >= before) & (key - before <= query))
    for h in range(q_ref.shape[1] // HD):
        head = slice(h * HD, (h + 1) * HD)
        keys = stacked((*prev_refs, *kv_refs), 0, slice(None), head)
        values = stacked((*prev_refs, *kv_refs), 1, slice(None), head)
        logits = dot_nt(keys, stacked(q_refs, slice(None), head)) * SCORE
        logits = jnp.where(allowed, logits, NEG)
        top = jnp.max(logits, axis=0, keepdims=True)
        expo = jnp.exp(logits - top)
        top_ref[h : h + 1] = top
        sum_ref[h : h + 1] = jnp.sum(expo, axis=0, keepdims=True)
        acc_ref[h] = dot_tn(values, expo.astype(BF16))


def late_body(count, *refs):
    q_refs, (prev_ref, acc_ref, top_ref, sum_ref, out_ref) = refs[:count], refs[count:]
    has_prev = lax.axis_index("seq") > 0
    heads = range(out_ref.shape[1] // HD)
    at_head = [slice(h * HD, (h + 1) * HD) for h in heads]
    logits = [
        jnp.where(has_prev, dot_nt(prev_ref[0, :, at], stacked(q_refs, slice(None), at)) * SCORE, NEG)
        for at in at_head
    ]
    highest = jnp.concatenate([jnp.max(x, axis=0, keepdims=True) for x in logits], axis=0)
    top = jnp.maximum(top_ref[...], highest)
    fade = jnp.exp(top_ref[...] - top)
    expo = [jnp.exp(logits[h] - top[h : h + 1]) for h in heads]
    sums = jnp.concatenate([jnp.sum(x, axis=0, keepdims=True) for x in expo], axis=0)
    inverse = 1.0 / (sum_ref[...] * fade + sums)
    fade = fade * inverse
    for h in heads:
        weights = (expo[h] * inverse[h : h + 1]).astype(BF16)
        total = acc_ref[h] * fade[h : h + 1] + dot_tn(prev_ref[1, :, at_head[h]], weights)
        out_ref[:, at_head[h]] = total.T.astype(BF16)


def tuned(lin_qkv, resid, w_out, w_qkv):
    rows, _, width = lin_qkv.shape
    nheads = width // HD
    group = nheads // 2
    full = w_out.shape[1]
    block = width // 2
    seq = lax.axis_index("seq")
    core = seq % 2
    shape = jax.ShapeDtypeStruct

    def shared(shares):
        edges = [rows * sum(shares[:i]) // sum(shares) for i in range(len(shares) + 1)]
        return list(zip(edges, edges[1:]))

    cuts, across, owns, ends, turns = (shared(x) for x in (FIRST, ACROSS, OWN, LAST, TURN))
    sizes = [b - a for a, b in cuts]
    last = len(cuts) - 1

    qkv = jnp.transpose(lin_qkv, (1, 0, 2))
    wqkv = jnp.transpose(w_qkv, (1, 0, 2))

    positions = seq * rows + jnp.arange(rows, dtype=jnp.int32)
    freq = 500000.0 ** (-(jnp.arange(HD // 2, dtype=F32) * 2.0 / HD))
    angle = positions.astype(F32)[:, None] * freq[None, :]
    cosine, sine = jnp.cos(angle), jnp.sin(angle)
    cos2 = jnp.concatenate([cosine, cosine], axis=1)
    sin2 = jnp.concatenate([-sine, sine], axis=1)

    with jax.named_scope("state"):
        states = shape((group, HD, HD), BF16)

        def state(other, after):
            return call(
                functools.partial(state_body, other), (in_hbm(qkv), after), states, [IN_HBM, ANYWHERE],
                (
                    pltpu.VMEM((rows, width // 2), BF16),
                    pltpu.VMEM((rows, width // 2), BF16),
                    pltpu.SemaphoreType.DMA((2,)),
                ),
                flops=rows * width * HD, moved=2 * rows * width,
            )

        send = state(True, qkv)
        keep = state(False, send)
        other = swapped(send, "seq", 1)
        chip_total = (keep.astype(F32) + other.astype(F32)).astype(BF16)
        by_x = swapped(chip_total, "seq", 2)
        by_y = swapped(chip_total, "seq", 4)
        by_xy = swapped(chip_total, "seq", 6)
    with jax.named_scope("intra"):
        columns = pltpu.VMEM((2, width, width), BF16)
        intra, q, w_other, w_mine = call(
            intra_body, (qkv, chip_total, cos2, sin2, in_hbm(w_out)),
            (shape((rows, width), F32), shape((rows, width), BF16), columns, columns),
            [ON_CHIP, ANYWHERE, ANYWHERE, ANYWHERE, IN_HBM], (pltpu.SemaphoreType.DMA((4,)),),
            flops=4 * rows * rows * width, moved=2 * width * full,
        )
        w_other, w_mine = in_vmem(w_other), in_vmem(w_mine)
    with jax.named_scope("prefix"):
        x_bit = ((seq // 2) % 2).astype(F32)
        y_bit = (seq // 4).astype(F32)
        chips = (
            by_x.astype(F32) * x_bit + by_y.astype(F32) * y_bit + by_xy.astype(F32) * y_bit
        )
        low = chips.astype(BF16)
        first_core = jnp.where(core == 0, keep, other)
        high = (chips + first_core.astype(F32)).astype(BF16)
        own_prefix = jnp.where(core == 0, low, high)
        other_prefix = swapped(jnp.where(core == 0, high, low), "seq", 1)

    scale = 1.0 / math.sqrt(HD * rows * lax.axis_size("seq"))
    halves = [shape((n, full // 2), BF16) for n in sizes]
    lin_scratch = pltpu.VMEM((rows, width), BF16)
    lin_inputs = (q, intra, own_prefix, other_prefix, w_other)
    with jax.named_scope("partials"):
        first_send = call(
            functools.partial(send_body, scale, cuts), lin_inputs, halves[0], scratch=(lin_scratch,),
            flops=sizes[0] * width * full, moved=width * full,
        )
        got = [lax.ppermute(first_send, "head", PAIR)]
        *made, w_here = call(
            functools.partial(mine_body, scale, cuts), (*lin_inputs, w_mine, resid, in_hbm(wqkv), first_send),
            (*halves[1:], *halves, pltpu.VMEM(wqkv.shape, BF16)),
            [ON_CHIP] * 7 + [IN_HBM, ANYWHERE], (lin_scratch, pltpu.SemaphoreType.DMA((3 * full // width,))),
            flops=2 * rows * width * full, moved=6 * width * full,
        )
        sends, mines = made[:last], made[last:]
        w_here = in_vmem(w_here)

    def added(lefts, rights, groups, target, after=()):
        places = overlaps(groups, target)
        ins = [x for i, _, _ in places for x in (lefts[i], rights[i])]
        out = shape((target[1] - target[0], full // 2), BF16)
        specs = [ON_CHIP] * len(ins) + [ANYWHERE] * len(after)
        return call(functools.partial(add_body, places), (*ins, *after), out, specs, vmem=4, moved=3 * out.size)

    with jax.named_scope("mix"):
        got += [lax.ppermute(send, "head", PAIR) for send in sends]
        sums, far = [], []
        for i, group in enumerate(across):
            part = added(mines, got, cuts, group, sums[-1:])
            for j in {2: (1,)}.get(i, ()):
                part, far[j] = lax.optimization_barrier((part, far[j]))
            sums.append(part)
            far.append(lax.ppermute(part, "head", CROSS))

    def inside(group):
        return [i for i, (a, b) in enumerate(ends) if group[0] <= a and b <= group[1]]

    totals, rests, accs = [], [], []
    queries, invs, kvs, prevs = [], [], [], []
    ring = [(i, (i + 1) % lax.axis_size("seq")) for i in range(lax.axis_size("seq"))]

    def turn(group):
        members = inside(group)
        (k, own, _), = overlaps(owns, group)
        n = group[1] - group[0]
        tail = k == len(owns) - 1
        kv, other = call(
            functools.partial(kv_body, block, group, own, len(members)),
            (*(totals[i] for i in members), *(rests[i] for i in members), w_here, accs[k], cos2, sin2, accs[-1]),
            (shape((2, n, width), BF16), shape((n, HD), F32) if tail else shape((n, width), BF16)),
            [ON_CHIP] * (2 * len(members) + 4) + [ANYWHERE],
        )
        kvs.append(kv)
        (invs if tail else queries).append(other)
        prevs.append(lax.ppermute(kv, "seq", ring))

    for k, group in enumerate(owns):
        members = inside(group)
        before = totals[-1:]
        if k == len(owns) - 1:
            with jax.named_scope("project"):
                for early in turns:
                    if early[1] <= owns[0][1]:
                        turn(early)
            before = kvs[-1:] and before
        with jax.named_scope("mix"):
            for i in members:
                totals.append(added(sums, far, across, ends[i], before))
            rests += [lax.ppermute(totals[i], "head", PAIR) for i in members]
        with jax.named_scope("project"):
            acc = shape((3, group[1] - group[0], width), F32)
            if k < len(owns) - 1:
                inputs = [totals[i] for i in members]
                accs.append(call(functools.partial(first_body, block), (w_here, *inputs), acc))
                continue
            acc, hidden = call(
                functools.partial(first_hidden_body, block, ends, len(members)), (w_here, *totals),
                (acc, shape((rows, width), BF16)),
            )
            accs.append(acc)
    with jax.named_scope("project"):
        for group in turns[len(kvs) :]:
            turn(group)
    with jax.named_scope("attend"):
        stat = shape((nheads, rows), F32)
        tail = owns[-1]
        members = [rests[i] for i in inside(tail)]
        query, acc, top, total = call(
            functools.partial(early_body, block, tail, turns[-1][0], len(queries), len(members), len(invs), len(kvs)),
            (w_here, accs[-1], cos2, sin2, *members, *invs, *queries, *kvs, *prevs[:-1]),
            (shape((tail[1] - tail[0], width), BF16), shape((nheads, HD, rows), F32), stat, stat),
            flops=8 * rows * rows * width, moved=12 * rows * width,
        )
        queries.append(query)
        attended = call(
            functools.partial(late_body, len(queries)), (*queries, prevs[-1], acc, top, total),
            shape((rows, width), BF16), flops=2 * rows * rows * width, moved=12 * rows * width,
        )
    return hidden, attended


def solution(mesh):
    line = mesh.shape["seq"] == 8 and mesh.shape["head"] == 4
    return jax.shard_map(
        tuned if line else general,
        mesh=mesh,
        in_specs=(P("seq", None, "head"), P("seq", "head"), P("head", None), P(None, None, "head")),
        out_specs=(P("seq", "head"), P("seq", "head")),
        check_vma=False,
    )
```

```python
import functools
import math

import jax
import jax.numpy as jnp
from jax import lax
from jax.experimental import pallas as pl
from jax.experimental.pallas import tpu as pltpu
from jax.sharding import PartitionSpec as P

D = 4096
HD = 128
BF16 = jnp.bfloat16
F32 = jnp.float32
NEG = -1e30
FIRST, ACROSS, OWN, LAST, TURN = (1, 1), (2, 1, 1), (2, 1, 1), (2, 1, 1), (2, 1, 1)

PAIR = [(0, 1), (1, 0), (2, 3), (3, 2)]
CROSS = [(0, 3), (3, 0), (1, 2), (2, 1)]


def shifted(array, axis, by):
    devices = lax.axis_size(axis)
    pairs = [(i, i + by) for i in range(devices) if 0 <= i + by < devices]
    return lax.ppermute(array, axis, pairs)


def swapped(array, axis, bits):
    return lax.ppermute(array, axis, [(i, i ^ bits) for i in range(lax.axis_size(axis))])


def rotary(values, positions):
    half = values.shape[-1] // 2
    freq = 500000.0 ** (-(jnp.arange(half, dtype=jnp.float32) * 2.0 / values.shape[-1]))
    angle = positions.astype(jnp.float32)[:, None] * freq[None, :]
    cosine = jnp.cos(angle)[:, None, :]
    sine = jnp.sin(angle)[:, None, :]
    first = values[..., :half]
    second = values[..., half:]
    return jnp.concatenate(
        [first * cosine - second * sine, second * cosine + first * sine], axis=-1
    )


def general(lin_qkv, resid, w_out, w_qkv):
    tok_rows = lin_qkv.shape[0]
    local_width = lin_qkv.shape[2]
    nheads = local_width // HD
    n_seq = lax.axis_size("seq")
    own_index = lax.axis_index("seq")
    queries = lin_qkv[:, 0].reshape(tok_rows, nheads, HD)
    keys = lin_qkv[:, 1].reshape(tok_rows, nheads, HD)
    values = lin_qkv[:, 2].reshape(tok_rows, nheads, HD)
    own_state = jnp.einsum("thd,the->hde", keys, values, preferred_element_type=jnp.float32)
    piece = lax.all_gather(own_state[None], "seq", axis=0, tiled=True)
    keep = (jnp.arange(piece.shape[0], dtype=jnp.int32) < own_index).astype(jnp.float32)
    before = jnp.sum(piece * keep[:, None, None, None], axis=0)
    before = before.astype(jnp.bfloat16)
    causal = jnp.tril(jnp.ones((tok_rows, tok_rows), dtype=bool))
    scores = jnp.einsum("thd,shd->hts", queries, keys, preferred_element_type=jnp.float32)
    inner = jnp.where(causal[None], scores, 0.0).astype(jnp.bfloat16)
    total = jnp.einsum("hts,shd->thd", inner, values, preferred_element_type=jnp.float32)
    total = total + jnp.einsum("thd,hde->the", queries, before, preferred_element_type=jnp.float32)
    scale = 1.0 / math.sqrt(HD * tok_rows * n_seq)
    lin_out = (total * scale).astype(jnp.bfloat16).reshape(tok_rows, local_width)
    shared = lax.psum_scatter(
        lax.dot_general(
            w_out, lin_out, (((0,), (1,)), ((), ())), preferred_element_type=jnp.float32
        ).astype(jnp.bfloat16),
        "head",
        scatter_dimension=0,
        tiled=True,
    ).astype(jnp.float32)
    mixed_f = resid.astype(jnp.float32) + shared.T
    hidden = mixed_f.astype(jnp.bfloat16)
    flat_w = w_qkv.reshape(w_qkv.shape[0], 3 * local_width)
    squared = lax.psum(jnp.sum(mixed_f * mixed_f, axis=1), "head")
    normed = (mixed_f * lax.rsqrt(squared[:, None] / D + 1e-05)).astype(jnp.bfloat16)
    proj = jnp.dot(
        lax.all_gather(normed, "head", axis=1, tiled=True),
        flat_w,
        preferred_element_type=jnp.float32,
    )
    proj = proj.reshape(tok_rows, 3, nheads, HD)
    positions = own_index * tok_rows + jnp.arange(tok_rows, dtype=jnp.int32)
    query2 = rotary(proj[:, 0], positions).astype(jnp.bfloat16)
    key2 = rotary(proj[:, 1], positions).astype(jnp.bfloat16)
    value2 = proj[:, 2].astype(jnp.bfloat16)
    key_prev, value_prev = shifted((key2, value2), "seq", 1)
    score_scale = 1.0 / math.sqrt(HD)
    all_keys = jnp.concatenate([key_prev, key2], axis=0)
    all_values = jnp.concatenate([value_prev, value2], axis=0)
    logits = (
        jnp.einsum("thd,shd->hts", query2, all_keys, preferred_element_type=jnp.float32)
        * score_scale
    )
    allowed = jnp.concatenate([jnp.full((tok_rows, tok_rows), own_index > 0), causal], axis=1)
    logits = jnp.where(allowed[None], logits, -1e30)
    top = jnp.max(logits, axis=2, keepdims=True)
    expo = jnp.where(allowed[None], jnp.exp(logits - top), 0.0)
    weights = (expo / jnp.sum(expo, axis=2, keepdims=True)).astype(jnp.bfloat16)
    attended = jnp.einsum("hts,shd->thd", weights, all_values, preferred_element_type=jnp.float32)
    return (hidden, attended.astype(jnp.bfloat16).reshape(tok_rows, local_width))


def dot(a, b):
    return jnp.dot(a, b, preferred_element_type=F32)


def dot_nt(a, b):
    return lax.dot_general(a, b, (((1,), (1,)), ((), ())), preferred_element_type=F32)


def dot_tn(a, b):
    return lax.dot_general(a, b, (((0,), (0,)), ((), ())), preferred_element_type=F32)


def at(start, size):
    return pl.ds(pl.multiple_of(start, size), size)


ON_CHIP = pl.BlockSpec(memory_space=pltpu.VMEM)
IN_HBM = pl.BlockSpec(memory_space=pltpu.HBM)
ANYWHERE = pl.BlockSpec(memory_space=pl.ANY)


def call(body, ins, outs, in_specs=None, scratch=(), vmem=8, flops=0, moved=0, cost=0):
    return pl.pallas_call(
        body,
        in_specs=in_specs or [ON_CHIP] * len(ins),
        out_specs=jax.tree.map(lambda _: ON_CHIP, outs),
        out_shape=outs,
        scratch_shapes=scratch,
        compiler_params=pltpu.CompilerParams(vmem_limit_bytes=vmem * 2**20),
        cost_estimate=pl.CostEstimate(flops=cost, bytes_accessed=0, transcendentals=0),
    )(*ins)


def start_all(pairs, sems):
    copies = [pltpu.make_async_copy(a, b, sems.at[i]) for i, (a, b) in enumerate(pairs)]
    for copy in copies:
        copy.start()
    return copies


def in_hbm(array):
    return pltpu.with_memory_space_constraint(array, pltpu.HBM)


def in_vmem(array):
    return pltpu.with_memory_space_constraint(array, pltpu.VMEM)


def state_body(other, qkv_ref, after, state_ref, k_ref, v_ref, sems):
    core = lax.axis_index("seq") % 2
    group = 1 - core if other else core
    wide = k_ref.shape[1]
    copies = start_all(
        [
            (qkv_ref.at[plane, :, at(group * wide, wide)], ref)
            for plane, ref in ((1, k_ref), (2, v_ref))
        ],
        sems,
    )
    for copy in copies:
        copy.wait()
    for j in range(state_ref.shape[0]):
        head = slice(j * HD, (j + 1) * HD)
        state_ref[j] = dot_tn(k_ref[:, head], v_ref[:, head]).astype(BF16)


def intra_body(qkv_ref, after, cos_ref, sin_ref, w_ref, o_ref, q_ref, w_other_ref, w_mine_ref, sems):
    _, mine, other = quarters()
    width = w_mine_ref.shape[2]
    copies = start_all(
        [
            (w_ref.at[:, at(which[p] * width, width)], to.at[p])
            for which, to in ((other, w_other_ref), (mine, w_mine_ref))
            for p in range(2)
        ],
        sems,
    )
    rows = qkv_ref.shape[1]
    ahead = lax.broadcasted_iota(jnp.int32, (rows, rows), 1) > lax.broadcasted_iota(
        jnp.int32, (rows, rows), 0
    )
    q_ref[...] = qkv_ref[0]
    for h in range(qkv_ref.shape[2] // HD):
        head = slice(h * HD, (h + 1) * HD)
        scores = dot_nt(qkv_ref[0, :, head], qkv_ref[1, :, head])
        inner = jnp.where(ahead, 0.0, scores).astype(BF16)
        o_ref[:, head] = dot(inner, qkv_ref[2, :, head])
    for copy in copies:
        copy.wait()


def quarters():
    z = lax.axis_index("head")
    edge = (z == 0) | (z == 3)
    outer, inner = (0, 3), (1, 2)
    mine = [jnp.where(edge, a, b) for a, b in zip(outer, inner)]
    other = [jnp.where(edge, b, a) for a, b in zip(outer, inner)]
    return z, mine, other


def lin_out_rows(scale, rows, q_ref, intra_ref, own_ref, other_ref, lin_ref):
    core = lax.axis_index("seq") % 2
    count = own_ref.shape[0]
    for ref, group in ((own_ref, core), (other_ref, 1 - core)):
        for j in range(count):
            head = at((group * count + j) * HD, HD)
            total = intra_ref[rows, head] + dot(q_ref[rows, head], ref[j])
            lin_ref[rows, head] = (total * scale).astype(BF16)


def send_body(scale, cuts, q_ref, intra_ref, own_ref, other_ref, w_ref, send_ref, lin_ref):
    rows = slice(*cuts[0])
    lin_out_rows(scale, rows, q_ref, intra_ref, own_ref, other_ref, lin_ref)
    width = w_ref.shape[2]
    block = width // 2
    for p in range(2):
        for n in range(2):
            to = slice(p * width + n * block, p * width + (n + 1) * block)
            send_ref[:, to] = dot(lin_ref[rows], w_ref[p, :, n * block : (n + 1) * block]).astype(BF16)


def mine_body(scale, cuts, *refs):
    q_ref, intra_ref, own_ref, other_ref, w_other_ref, w_mine_ref, r_ref, w_qkv_ref, after = refs[:9]
    count = len(cuts)
    send_refs, mine_refs = refs[9 : 8 + count], refs[8 + count : 8 + 2 * count]
    w_qkv_to_ref, lin_ref, sems = refs[8 + 2 * count :]
    z, mine, _ = quarters()
    width = w_mine_ref.shape[2]
    block = width // 2
    copies = start_all(
        [
            (w_qkv_ref.at[j, pl.ds(i, width)], w_qkv_to_ref.at[j, pl.ds(i, width)])
            for j in range(3)
            for i in range(0, w_qkv_ref.shape[1], width)
        ],
        sems,
    )
    lin_out_rows(scale, slice(None), q_ref, intra_ref, own_ref, other_ref, lin_ref)
    skip = cuts[0][1]
    for p in range(2):
        for n in range(2):
            part = slice(n * block, (n + 1) * block)
            to = slice(p * width + n * block, p * width + (n + 1) * block)
            product = dot(lin_ref[skip:], w_other_ref[p, :, part]).astype(BF16)
            for (a, b), ref in zip(cuts[1:], send_refs):
                ref[:, to] = product[a - skip : b - skip]
    for p in range(2):
        for n in range(2):
            part = slice(n * block, (n + 1) * block)
            to = slice(p * width + n * block, p * width + (n + 1) * block)
            product = dot(lin_ref[...], w_mine_ref[p, :, part])
            own = jnp.where(mine[p] == z, r_ref[:, part].astype(F32), 0.0)
            product = (product + own).astype(BF16)
            for (a, b), ref in zip(cuts, mine_refs):
                ref[:, to] = product[a:b]
    for copy in copies:
        copy.wait()


def overlaps(groups, rows):
    found = []
    for i, (a, b) in enumerate(groups):
        low, high = max(a, rows[0]), min(b, rows[1])
        if low < high:
            found.append((i, slice(low - a, high - a), slice(low - rows[0], high - rows[0])))
    return found


def add_body(places, *refs):
    *refs, o_ref = refs
    for i, (_, source, target) in enumerate(places):
        total = refs[2 * i][source].astype(F32) + refs[2 * i + 1][source].astype(F32)
        o_ref[target] = total.astype(BF16)


def two_quarters(x, w_ref, plane, which, to):
    width = x.shape[1] // 2
    low = dot(x[:, :width], w_ref[plane, at(which[0] * width, width), to])
    return low + dot(x[:, width:], w_ref[plane, at(which[1] * width, width), to])


def joined(refs):
    return refs[0] if len(refs) == 1 else jnp.concatenate([ref[...] for ref in refs], axis=0)


def first_body(block, w_ref, *refs):
    *x_refs, acc_ref = refs
    _, mine, _ = quarters()
    x = joined(x_refs)
    for plane in range(3):
        for n in range(acc_ref.shape[2] // block):
            to = slice(n * block, (n + 1) * block)
            acc_ref[plane, :, to] = two_quarters(x, w_ref, plane, mine, to)


def hidden_body(cuts, *refs):
    *total_refs, hidden_ref = refs
    width = hidden_ref.shape[1]
    own = at((lax.axis_index("head") // 2) * width, width)
    for (a, b), ref in zip(cuts, total_refs):
        hidden_ref[a:b] = ref[:, own]


def finish(block, plane, x, w_ref, acc_ref, rows, inv, cos, sin, out_ref):
    _, _, other = quarters()
    for n in range(acc_ref.shape[2] // block):
        to = slice(n * block, (n + 1) * block)
        total = (acc_ref[plane, rows, to] + two_quarters(x, w_ref, plane, other, to)) * inv
        if plane == 2:
            out_ref[:, to] = total.astype(BF16)
            continue
        for h in range(block // HD):
            value = total[:, h * HD : (h + 1) * HD]
            turned = value * cos + pltpu.roll(value, HD // 2, 1) * sin
            out_ref[:, n * block + h * HD : n * block + (h + 1) * HD] = turned.astype(BF16)


def kv_body(block, rows, own, count, *refs):
    t_refs, x_refs = refs[:count], refs[count : 2 * count]
    w_ref, acc_ref, cos_ref, sin_ref, _, kv_ref, rest_ref = refs[2 * count :]
    x_ref = joined(x_refs)
    t = joined(t_refs)[...].astype(F32)
    x = x_ref[...].astype(F32)
    total = jnp.sum(t * t + x * x, axis=1, keepdims=True)
    inv = lax.rsqrt(total / D + 1e-05)
    cos, sin = cos_ref[slice(*rows)], sin_ref[slice(*rows)]
    for plane in (1, 2):
        finish(block, plane, x_ref, w_ref, acc_ref, own, inv, cos, sin, kv_ref.at[plane - 1])
    if rest_ref.dtype == BF16:
        finish(block, 0, x_ref, w_ref, acc_ref, own, inv, cos, sin, rest_ref)
    else:
        rest_ref[...] = jnp.broadcast_to(inv, rest_ref.shape)


SCORE = 1.0 / math.sqrt(HD)


def stacked(refs, *where):
    return jnp.concatenate([ref[where] for ref in refs], axis=0)


def early_body(block, rows, before, q_count, x_count, inv_count, kv_count, *refs):
    w_ref, acc_in_ref, cos_ref, sin_ref = refs[:4]
    refs = refs[4:]
    x_refs, refs = refs[:x_count], refs[x_count:]
    inv_refs, refs = refs[:inv_count], refs[inv_count:]
    q_refs, refs = refs[:q_count], refs[q_count:]
    kv_refs, prev_refs = refs[:kv_count], refs[kv_count : 2 * kv_count - 1]
    q_ref, acc_ref, top_ref, sum_ref = refs[2 * kv_count - 1 :]
    inv = joined(inv_refs)[:, :1]
    cos, sin = cos_ref[slice(*rows)], sin_ref[slice(*rows)]
    finish(block, 0, joined(x_refs), w_ref, acc_in_ref, slice(None), inv, cos, sin, q_ref)
    q_refs = (*q_refs, q_ref)
    has_prev = lax.axis_index("seq") > 0
    shape = (before + rows[1], rows[1])
    key = lax.broadcasted_iota(jnp.int32, shape, 0)
    query = lax.broadcasted_iota(jnp.int32, shape, 1)
    allowed = ((key < before) & has_prev) | ((key >= before) & (key - before <= query))
    for h in range(q_ref.shape[1] // HD):
        head = slice(h * HD, (h + 1) * HD)
        keys = stacked((*prev_refs, *kv_refs), 0, slice(None), head)
        values = stacked((*prev_refs, *kv_refs), 1, slice(None), head)
        logits = dot_nt(keys, stacked(q_refs, slice(None), head)) * SCORE
        logits = jnp.where(allowed, logits, NEG)
        top = jnp.max(logits, axis=0, keepdims=True)
        expo = jnp.exp(logits - top)
        top_ref[h : h + 1] = top
        sum_ref[h : h + 1] = jnp.sum(expo, axis=0, keepdims=True)
        acc_ref[h] = dot_tn(values, expo.astype(BF16))


def late_body(count, *refs):
    q_refs, (prev_ref, acc_ref, top_ref, sum_ref, out_ref) = refs[:count], refs[count:]
    has_prev = lax.axis_index("seq") > 0
    heads = range(out_ref.shape[1] // HD)
    at_head = [slice(h * HD, (h + 1) * HD) for h in heads]
    logits = [
        jnp.where(has_prev, dot_nt(prev_ref[0, :, at], stacked(q_refs, slice(None), at)) * SCORE, NEG)
        for at in at_head
    ]
    highest = jnp.concatenate([jnp.max(x, axis=0, keepdims=True) for x in logits], axis=0)
    top = jnp.maximum(top_ref[...], highest)
    fade = jnp.exp(top_ref[...] - top)
    expo = [jnp.exp(logits[h] - top[h : h + 1]) for h in heads]
    sums = jnp.concatenate([jnp.sum(x, axis=0, keepdims=True) for x in expo], axis=0)
    inverse = 1.0 / (sum_ref[...] * fade + sums)
    fade = fade * inverse
    for h in heads:
        weights = (expo[h] * inverse[h : h + 1]).astype(BF16)
        total = acc_ref[h] * fade[h : h + 1] + dot_tn(prev_ref[1, :, at_head[h]], weights)
        out_ref[:, at_head[h]] = total.T.astype(BF16)


def tuned(lin_qkv, resid, w_out, w_qkv):
    rows, _, width = lin_qkv.shape
    nheads = width // HD
    group = nheads // 2
    full = w_out.shape[1]
    block = width // 2
    seq = lax.axis_index("seq")
    core = seq % 2
    shape = jax.ShapeDtypeStruct

    def shared(shares):
        edges = [rows * sum(shares[:i]) // sum(shares) for i in range(len(shares) + 1)]
        return list(zip(edges, edges[1:]))

    cuts, across, owns, ends, turns = (shared(x) for x in (FIRST, ACROSS, OWN, LAST, TURN))
    sizes = [b - a for a, b in cuts]
    last = len(cuts) - 1

    qkv = jnp.transpose(lin_qkv, (1, 0, 2))
    wqkv = jnp.transpose(w_qkv, (1, 0, 2))

    positions = seq * rows + jnp.arange(rows, dtype=jnp.int32)
    freq = 500000.0 ** (-(jnp.arange(HD // 2, dtype=F32) * 2.0 / HD))
    angle = positions.astype(F32)[:, None] * freq[None, :]
    cosine, sine = jnp.cos(angle), jnp.sin(angle)
    cos2 = jnp.concatenate([cosine, cosine], axis=1)
    sin2 = jnp.concatenate([-sine, sine], axis=1)

    with jax.named_scope("state"):
        states = shape((group, HD, HD), BF16)

        def state(other, after):
            return call(
                functools.partial(state_body, other), (in_hbm(qkv), after), states, [IN_HBM, ANYWHERE],
                (
                    pltpu.VMEM((rows, width // 2), BF16),
                    pltpu.VMEM((rows, width // 2), BF16),
                    pltpu.SemaphoreType.DMA((2,)),
                ),
                flops=rows * width * HD, moved=2 * rows * width,
            )

        send = state(True, qkv)
        keep = state(False, send)
        other = swapped(send, "seq", 1)
        chip_total = (keep.astype(F32) + other.astype(F32)).astype(BF16)
        by_x = swapped(chip_total, "seq", 2)
        by_y = swapped(chip_total, "seq", 4)
        by_xy = swapped(chip_total, "seq", 6)
    with jax.named_scope("intra"):
        columns = pltpu.VMEM((2, width, width), BF16)
        intra, q, w_other, w_mine = call(
            intra_body, (qkv, chip_total, cos2, sin2, in_hbm(w_out)),
            (shape((rows, width), F32), shape((rows, width), BF16), columns, columns),
            [ON_CHIP, ANYWHERE, ANYWHERE, ANYWHERE, IN_HBM], (pltpu.SemaphoreType.DMA((4,)),),
            flops=4 * rows * rows * width, moved=2 * width * full,
        )
        w_other, w_mine = in_vmem(w_other), in_vmem(w_mine)
    with jax.named_scope("prefix"):
        x_bit = ((seq // 2) % 2).astype(F32)
        y_bit = (seq // 4).astype(F32)
        chips = (
            by_x.astype(F32) * x_bit + by_y.astype(F32) * y_bit + by_xy.astype(F32) * y_bit
        )
        low = chips.astype(BF16)
        first_core = jnp.where(core == 0, keep, other)
        high = (chips + first_core.astype(F32)).astype(BF16)
        own_prefix = jnp.where(core == 0, low, high)
        other_prefix = swapped(jnp.where(core == 0, high, low), "seq", 1)

    scale = 1.0 / math.sqrt(HD * rows * lax.axis_size("seq"))
    halves = [shape((n, full // 2), BF16) for n in sizes]
    lin_scratch = pltpu.VMEM((rows, width), BF16)
    lin_inputs = (q, intra, own_prefix, other_prefix, w_other)
    with jax.named_scope("partials"):
        first_send = call(
            functools.partial(send_body, scale, cuts), lin_inputs, halves[0], scratch=(lin_scratch,),
            flops=sizes[0] * width * full, moved=width * full,
        )
        got = [lax.ppermute(first_send, "head", PAIR)]
        *made, w_here = call(
            functools.partial(mine_body, scale, cuts), (*lin_inputs, w_mine, resid, in_hbm(wqkv), first_send),
            (*halves[1:], *halves, pltpu.VMEM(wqkv.shape, BF16)),
            [ON_CHIP] * 7 + [IN_HBM, ANYWHERE], (lin_scratch, pltpu.SemaphoreType.DMA((3 * full // width,))),
            flops=2 * rows * width * full, moved=6 * width * full,
        )
        sends, mines = made[:last], made[last:]
        w_here = in_vmem(w_here)

    def added(lefts, rights, groups, target, after=()):
        places = overlaps(groups, target)
        ins = [x for i, _, _ in places for x in (lefts[i], rights[i])]
        out = shape((target[1] - target[0], full // 2), BF16)
        specs = [ON_CHIP] * len(ins) + [ANYWHERE] * len(after)
        return call(functools.partial(add_body, places), (*ins, *after), out, specs, vmem=4, moved=3 * out.size)

    with jax.named_scope("mix"):
        got += [lax.ppermute(send, "head", PAIR) for send in sends]
        sums, far = [], []
        for i, group in enumerate(across):
            part = added(mines, got, cuts, group, sums[-1:])
            for j in {2: (1,)}.get(i, ()):
                part, far[j] = lax.optimization_barrier((part, far[j]))
            sums.append(part)
            far.append(lax.ppermute(part, "head", CROSS))

    def inside(group):
        return [i for i, (a, b) in enumerate(ends) if group[0] <= a and b <= group[1]]

    totals, rests, accs = [], [], []
    queries, invs, kvs, prevs = [], [], [], []
    ring = [(i, (i + 1) % lax.axis_size("seq")) for i in range(lax.axis_size("seq"))]

    def turn(group):
        members = inside(group)
        (k, own, _), = overlaps(owns, group)
        n = group[1] - group[0]
        tail = k == len(owns) - 1
        kv, other = call(
            functools.partial(kv_body, block, group, own, len(members)),
            (*(totals[i] for i in members), *(rests[i] for i in members), w_here, accs[k], cos2, sin2, accs[-1]),
            (shape((2, n, width), BF16), shape((n, HD), F32) if tail else shape((n, width), BF16)),
            [ON_CHIP] * (2 * len(members) + 4) + [ANYWHERE],
        )
        kvs.append(kv)
        (invs if tail else queries).append(other)
        prevs.append(lax.ppermute(kv, "seq", ring))

    for k, group in enumerate(owns):
        members = inside(group)
        before = totals[-1:]
        if k == len(owns) - 1:
            with jax.named_scope("project"):
                for early in turns:
                    if early[1] <= owns[0][1]:
                        turn(early)
            before = kvs[-1:] and before
        with jax.named_scope("mix"):
            for i in members:
                totals.append(added(sums, far, across, ends[i], before))
            rests += [lax.ppermute(totals[i], "head", PAIR) for i in members]
        with jax.named_scope("project"):
            acc = shape((3, group[1] - group[0], width), F32)
            if k < len(owns) - 1:
                inputs = [totals[i] for i in members]
                accs.append(call(functools.partial(first_body, block), (w_here, *inputs), acc))
                continue
            inputs = [totals[i] for i in members]
            accs.append(call(functools.partial(first_body, block), (w_here, *inputs), acc))
            hidden = call(functools.partial(hidden_body, ends), totals, shape((rows, width), BF16))
    with jax.named_scope("project"):
        for group in turns[len(kvs) :]:
            turn(group)
    with jax.named_scope("attend"):
        stat = shape((nheads, rows), F32)
        tail = owns[-1]
        members = [rests[i] for i in inside(tail)]
        query, acc, top, total = call(
            functools.partial(early_body, block, tail, turns[-1][0], len(queries), len(members), len(invs), len(kvs)),
            (w_here, accs[-1], cos2, sin2, *members, *invs, *queries, *kvs, *prevs[:-1]),
            (shape((tail[1] - tail[0], width), BF16), shape((nheads, HD, rows), F32), stat, stat),
            flops=8 * rows * rows * width, moved=12 * rows * width,
        )
        queries.append(query)
        attended = call(
            functools.partial(late_body, len(queries)), (*queries, prevs[-1], acc, top, total),
            shape((rows, width), BF16), flops=2 * rows * rows * width, moved=12 * rows * width,
        )
    return hidden, attended


def solution(mesh):
    line = mesh.shape["seq"] == 8 and mesh.shape["head"] == 4
    return jax.shard_map(
        tuned if line else general,
        mesh=mesh,
        in_specs=(P("seq", None, "head"), P("seq", "head"), P("head", None), P(None, None, "head")),
        out_specs=(P("seq", "head"), P("seq", "head")),
        check_vma=False,
    )
```
